128 devices in a mesh: ctx: 32 (over y, z, core), exp: 4 (over x).
Axes of the slice: x: 4, y: 4, z: 4, core: 2. Of those that a mesh axis runs over, the one named last changes fastest.
Arguments:
- queries: bfloat16 [4096, 6144], P('ctx', 'exp'), may hold values from -0.3984375 to 0.3984375
- keys: bfloat16 [4096, 6144], P('ctx', 'exp'), may hold values from -0.3984375 to 0.3984375
- values: bfloat16 [4096, 6144], P('ctx', 'exp'), may hold values from -0.3984375 to 0.3984375
- log_decay: float32 [48, 4096], P('exp', 'ctx'), may hold values from -1 to 0, as said below
- moe_input: bfloat16 [4096, 6144], P('ctx', 'exp'), may hold values from -6 to 6
- out_grad: bfloat16 [4096, 6144], P('ctx', 'exp'), may hold values from -6 to 6
- expert_ids: int32 [4096, 2], P('ctx'), may hold values from 0 to 31, all different within a row; in each aligned block of 128 rows (0 to 127, 128 to 255, ...) at most 9 rows name the same one
- route_gates: float32 [4096, 2], P('ctx'), may hold values from 0.2 to 1
- w_gate: bfloat16 [4, 6144, 8192], P('exp', None, 'ctx'), may hold values from -0.078125 to 0.078125
- w_up: bfloat16 [4, 6144, 8192], P('exp', None, 'ctx'), may hold values from -0.078125 to 0.078125
- w_down: bfloat16 [4, 8192, 6144], P('exp', 'ctx'), may hold values from -0.0625 to 0.0625
Outputs:
- query_grad: bfloat16 [4096, 6144], P('ctx', 'exp')
- key_grad: bfloat16 [4096, 6144], P('ctx', 'exp')
- value_grad: bfloat16 [4096, 6144], P('ctx', 'exp')
- gate_grad: bfloat16 [4, 6144, 8192], P('exp', None, 'ctx')
- up_grad: bfloat16 [4, 6144, 8192], P('exp', None, 'ctx')
- down_grad: bfloat16 [4, 8192, 6144], P('exp', 'ctx')
The draws below stay inside these ranges and needn't reach their ends.
Inputs may be any that keep to these rules, and one draw needn't show every extreme that they name: `expert_ids`: each row names 2 different experts. In each aligned block of 128 rows (the rows of one index of ctx) no expert is named by more than 9 rows. `log_decay`: every entry is negative.
All inputs are finite; a program needn't handle non-finite values.
Results may differ from the reference program's by a relative error of at most 0.02.
Values may be sent and summed in bfloat16 or wider, within the bound.
A program may use at most 192 MiB of HBM per device.

```python
import math
import jax
import jax.numpy as jnp
import numpy as np
from jax import lax

EXPERTS = 32
TOP = 2
HEAD_DIM = 128
ACTIVE_HEADS = 48
FF = 8192
SEQ_DEV = 128
D = 6144
SEQUENCE_LENGTH = 4096
CAP = 9
IN_FLIGHT = 4
N_CTX = 32


def draw_log_decay(key, part):
    key = jax.random.fold_in(key, 11)
    key_collection = jax.random.split(key, 7)
    fast_share = 0.5
    fast_heads = jax.random.uniform(key_collection[0], (ACTIVE_HEADS, 1)) < fast_share
    slow_rate = jnp.exp(jax.random.uniform(key_collection[1], (ACTIVE_HEADS, 1), minval=jnp.log(0.15), maxval=jnp.log(1.0))) / SEQUENCE_LENGTH
    fast_rate = jnp.exp(jax.random.uniform(key_collection[2], (ACTIVE_HEADS, 1), minval=jnp.log(1.0 / 45.0), maxval=jnp.log(1.0 / 25.0)))
    decay_speed = jnp.where(fast_heads, fast_rate, slow_rate)
    block_count = SEQUENCE_LENGTH // SEQ_DEV
    block_multiplier = jnp.exp(jax.random.uniform(key_collection[3], (ACTIVE_HEADS, block_count, 1), minval=-0.7, maxval=0.7))
    block_multiplier = jnp.broadcast_to(block_multiplier, (ACTIVE_HEADS, block_count, SEQ_DEV)).reshape(ACTIVE_HEADS, SEQUENCE_LENGTH)
    jaggedness = jnp.exp(jax.random.uniform(key_collection[4], (ACTIVE_HEADS, SEQUENCE_LENGTH), minval=-0.5, maxval=0.5))
    position_indices = jax.random.randint(key_collection[5], (2, 1), 0, SEQUENCE_LENGTH)
    surge_mask = jnp.any(jnp.arange(SEQUENCE_LENGTH)[None, :] == position_indices, axis=0)
    surge_extent = jnp.log(jax.random.uniform(key_collection[6], (ACTIVE_HEADS, SEQUENCE_LENGTH), minval=0.55, maxval=0.8))
    return (-decay_speed * block_multiplier * jaggedness + jnp.where(surge_mask[None, :], surge_extent, 0.0)).astype(jnp.float32)


def shard_levels(rng, shape, shards, low, largest):
    loudness = 1.0
    for axis_at, blocks in shards:
        draws = jax.random.uniform(jax.random.fold_in(jax.random.fold_in(rng, 6), axis_at), (blocks,), jnp.float32, low / len(shards), largest / len(shards))
        loudness = loudness * jnp.repeat(jnp.exp(draws), shape[axis_at] // blocks).reshape((-1,) + (1,) * (len(shape) - 1 - axis_at))
    return loudness


def routed_block(rng, own, number, rows, count, top, limit, skew):
    sequence = jax.random.permutation(rng, count)
    packed, common = load_shares(count, rows * top, limit, skew, True), load_shares(count, rows * top, limit, skew, False)
    places = jnp.arange(count)

    def named(lengths, offset_by):
        used = int((lengths > 0).sum())
        fixed = max(1, used // 4)
        passed = fixed + (places - fixed + offset_by * (used - fixed)) % max(1, count - fixed)
        return jnp.zeros((count,), jnp.int32).at[sequence[jnp.where(places < fixed, places, passed)]].set(jnp.asarray(lengths, jnp.int32))

    lengths = jnp.where(number % 4 == 0, named(packed, number // 4), named(common, number - number // 4 - 1))
    mixed = jax.random.permutation(jax.random.fold_in(own, 3), count)
    source_of, sink = mixed[0:count // 2 * 2:2], mixed[1:count // 2 * 2:2]
    margin = jnp.minimum(lengths[source_of] - 1, limit - lengths[sink]) // 2
    margin = jnp.where((source_of == sequence[0]) | (sink == sequence[0]) | (lengths[sink] == 0), 0, jnp.maximum(margin, 0))
    passed = jax.random.randint(jax.random.fold_in(own, 4), (count // 2,), 0, 1 << 20) % (margin + 1)
    lengths = lengths.at[source_of].add(-passed).at[sink].add(passed)
    labels = jnp.searchsorted(jnp.cumsum(lengths), jnp.arange(rows * top), side="right").astype(jnp.int32)
    listing = labels.reshape(top, rows).T
    listing = listing[jax.random.permutation(jax.random.fold_in(own, 1), rows)]
    offset_by = jax.random.randint(jax.random.fold_in(own, 2), (rows, 1), 0, top)
    return jnp.take_along_axis(listing, (jnp.arange(top)[None, :] + offset_by) % top, axis=1)


def load_shares(number_of, total, reach, skew, full):
    weights = [(1 << 20) // math.isqrt(standing ** skew) + 1 for standing in range(1, number_of + 1)]
    largest = reach if full else min(reach, max(-(-total // number_of), total * weights[0] // sum(weights)))
    least = 1 if total - largest >= number_of - 1 else 0
    holding, spare = [largest] + [least] * (number_of - 1), total - largest - least * (number_of - 1)
    while spare > 0:
        candidates = [i for i in range(1, number_of) if holding[i] < largest] or [i for i in range(1, number_of) if holding[i] < reach]
        mass, left = sum([weights[i] for i in candidates]), spare
        for i in candidates:
            more = min(reach - holding[i], max(1, left * weights[i] // mass), spare)
            holding[i] = holding[i] + more
            spare = spare - more
    return np.array(holding)


def gaussian(own_key, dims, scale, limit, pieces=(), kind=jnp.bfloat16):
    result = jax.random.normal(own_key, dims, jnp.float32) * scale
    if len(pieces) > 0:
        result = shard_levels(own_key, dims, pieces, -0.22, 0.18) * result
    return jnp.clip(result, min=-limit, max=limit).astype(kind)


def setup_inputs(seed: int = 0) -> dict:
    key_of = jax.random.split(jax.random.key(seed), 12)
    queries = gaussian(key_of[0], (SEQUENCE_LENGTH, D), 0.06, 0.3984375, ((0, 32), (1, 4)))
    keys = gaussian(key_of[1], (SEQUENCE_LENGTH, D), 0.06, 0.3984375, ((0, 32), (1, 4)))
    values = gaussian(key_of[2], (SEQUENCE_LENGTH, D), 0.06, 0.3984375, ((0, 32), (1, 4)))
    log_decay = draw_log_decay(jax.random.fold_in(key_of[11], 71), 0)
    moe_input = gaussian(key_of[4], (SEQUENCE_LENGTH, D), 1.0, 6.0, ((0, 32), (1, 4)))
    out_grad = gaussian(key_of[5], (SEQUENCE_LENGTH, D), 1.0, 6.0, ((0, 32), (1, 4)))
    expert_ids_keys = jax.random.split(jax.random.fold_in(key_of[6], 1), SEQUENCE_LENGTH // SEQ_DEV)
    expert_ids_turns = jax.random.permutation(jax.random.fold_in(key_of[6], 3), SEQUENCE_LENGTH // SEQ_DEV)
    expert_ids = jax.vmap(lambda own, number: routed_block(jax.random.fold_in(key_of[6], 2), own, number, SEQ_DEV, EXPERTS, TOP, CAP, 2))(expert_ids_keys, expert_ids_turns).reshape((SEQUENCE_LENGTH, TOP))
    route_gates = jnp.clip(0.2 + 0.8 * jax.random.uniform(key_of[7], (SEQUENCE_LENGTH, TOP), jnp.float32) ** shard_levels(key_of[7], (SEQUENCE_LENGTH, TOP), ((0, 32),), -0.2, 0.2), 0.2, 1.0)
    w_gate = gaussian(key_of[8], (IN_FLIGHT, D, FF), D ** -0.5, 0.078125, ((0, 4), (2, 32)))
    w_up = gaussian(key_of[9], (IN_FLIGHT, D, FF), D ** -0.5, 0.078125, ((0, 4), (2, 32)))
    w_down = gaussian(key_of[10], (IN_FLIGHT, FF, D), FF ** -0.5, 0.0625, ((0, 4), (1, 32)))
    return {"queries": queries, "keys": keys, "values": values, "log_decay": log_decay, "moe_input": moe_input, "out_grad": out_grad, "expert_ids": expert_ids, "route_gates": route_gates, "w_gate": w_gate, "w_up": w_up, "w_down": w_down}


def multiply(form, left, right):
    return jnp.einsum(form, left.astype(jnp.float32), right.astype(jnp.float32))


def route_places(expert_ids, flight):
    flat_ids = expert_ids.reshape(-1)
    owners = jnp.arange(flight, dtype=jnp.int32)
    onehot = (flat_ids[:, None] == owners[None, :]).astype(jnp.float32)
    before = jnp.cumsum(onehot, axis=0) - onehot
    slot_rank = jnp.sum(before * onehot, axis=1).astype(jnp.int32)
    live_route = jnp.sum(onehot, axis=1) > 0.5
    places = jnp.where(live_route, flat_ids * CAP + slot_rank, -1).astype(jnp.int32)
    return places.reshape(expert_ids.shape)


def selectors(places, flight):
    slot_ids = jnp.arange(flight * CAP, dtype=jnp.int32)
    return [(places[:, route_index][None, :] == slot_ids[:, None]).astype(jnp.bfloat16) for route_index in range(TOP)]


def dispatch(pickers, sources):
    summed = jnp.zeros((pickers[0].shape[0], sources[0].shape[1]), jnp.float32)
    for chooser, source in zip(pickers, sources):
        summed = summed + jnp.dot(chooser, source, preferred_element_type=jnp.float32)
    return summed.astype(jnp.bfloat16)


def combine_back(pickers, slots_back, base_grad):
    summed = base_grad.astype(jnp.float32)
    for chooser in pickers:
        summed = summed + lax.dot_general(chooser, slots_back, (((0,), (0,)), ((), ())), preferred_element_type=jnp.float32)
    return summed.astype(jnp.bfloat16)


def expert_backward(inputs, grads, gate_w, up_w, down_w):
    gate_pre = jnp.dot(inputs, gate_w, preferred_element_type=jnp.float32)
    up_pre = jnp.dot(inputs, up_w, preferred_element_type=jnp.float32)
    sigmoid_gate = jax.nn.sigmoid(gate_pre)
    active = gate_pre * sigmoid_gate
    hidden = (active * up_pre).astype(jnp.bfloat16)
    hidden_grad = lax.dot_general(grads, down_w, (((1,), (1,)), ((), ())), preferred_element_type=jnp.float32)
    down_part = lax.dot_general(hidden, grads, (((0,), (0,)), ((), ())), preferred_element_type=jnp.float32).astype(jnp.bfloat16)
    gate_act = (hidden_grad * up_pre * sigmoid_gate * (1.0 + gate_pre * (1.0 - sigmoid_gate))).astype(jnp.bfloat16)
    up_act = (hidden_grad * active).astype(jnp.bfloat16)
    gate_part = lax.dot_general(inputs, gate_act, (((0,), (0,)), ((), ())), preferred_element_type=jnp.float32).astype(jnp.bfloat16)
    up_part = lax.dot_general(inputs, up_act, (((0,), (0,)), ((), ())), preferred_element_type=jnp.float32).astype(jnp.bfloat16)
    return gate_act, up_act, gate_part, up_part, down_part


def decay_tables(decay):
    running = jnp.cumsum(decay, axis=1)
    block_total = running[:, -1]
    length = decay.shape[1]
    lower = (jnp.arange(length)[:, None] >= jnp.arange(length)[None, :])[None]
    spread = running[:, :, None] - running[:, None, :]
    weights = jnp.where(lower, jnp.exp(jnp.where(lower, spread, 0.0)), 0.0)
    return running, block_total, weights


def local_state(block_total, running, key_half, value_half):
    scale = jnp.exp(block_total[:, None] - running).T[:, :, None]
    decayed = (scale * key_half.astype(jnp.float32)).astype(jnp.bfloat16)
    return multiply('shd,she->hde', decayed, value_half)


def grad_state(running, query_half, grad_half):
    decayed = (jnp.exp(running).T[:, :, None] * query_half.astype(jnp.float32)).astype(jnp.bfloat16)
    return multiply('thd,the->hde', decayed, grad_half)


def block_grads(weights, running, block_total, query_half, key_half, value_half, grad_half, state_in, state_grad):
    mixed = (multiply('the,she->hts', grad_half, value_half) * weights).astype(jnp.bfloat16)
    scores = (multiply('thd,shd->hts', query_half, key_half) * weights).astype(jnp.bfloat16)
    front = jnp.exp(running).T[:, :, None]
    tail = jnp.exp(block_total[:, None] - running).T[:, :, None]
    q_grad = multiply('hts,shd->thd', mixed, key_half) + front * multiply('the,hde->thd', grad_half, state_in)
    k_grad = multiply('hts,thd->shd', mixed, query_half) + tail * multiply('she,hde->shd', value_half, state_grad)
    v_grad = multiply('hts,the->she', scores, grad_half) + tail * multiply('shd,hde->she', key_half, state_grad)
    return q_grad, k_grad, v_grad


def reference(queries, keys, values, log_decay, moe_input, out_grad, expert_ids, route_gates, w_gate, w_up, w_down):
    flight = IN_FLIGHT
    block_count = N_CTX
    id_blocks = expert_ids.reshape(block_count, SEQ_DEV, TOP)
    input_blocks = moe_input.reshape(block_count, SEQ_DEV, D)
    grad_blocks = out_grad.reshape(block_count, SEQ_DEV, D)
    gate_blocks = route_gates.reshape(block_count, SEQ_DEV, TOP)

    def gather_block(block_item):
        block_ids, block_inputs, block_grads_in, block_gates = block_item
        pickers = selectors(route_places(block_ids, flight), flight)
        scaled = [(block_gates[:, route_index:route_index + 1] * block_grads_in).astype(jnp.bfloat16) for route_index in range(TOP)]
        return dispatch(pickers, [block_inputs] * TOP), dispatch(pickers, scaled)

    slot_inputs, slot_grads = lax.map(gather_block, (id_blocks, input_blocks, grad_blocks, gate_blocks))
    slot_inputs = slot_inputs.reshape(block_count, flight, CAP, D).transpose(1, 0, 2, 3).reshape(flight, block_count * CAP, D)
    slot_grads = slot_grads.reshape(block_count, flight, CAP, D).transpose(1, 0, 2, 3).reshape(flight, block_count * CAP, D)

    group_size = FF // N_CTX
    offsets = (jnp.arange(N_CTX) * group_size).astype(jnp.int32)
    gate_list, up_list, down_list, back_list = [], [], [], []
    for expert in range(flight):
        gate_w = w_gate[expert]
        up_w = w_up[expert]
        gate_act, up_act, gate_part, up_part, down_part = expert_backward(slot_inputs[expert], slot_grads[expert], gate_w, up_w, w_down[expert])

        def add_group(running_sum, offset):
            gate_cols = lax.dynamic_slice_in_dim(gate_act, offset, group_size, 1)
            up_cols = lax.dynamic_slice_in_dim(up_act, offset, group_size, 1)
            gate_block = lax.dynamic_slice_in_dim(gate_w, offset, group_size, 1)
            up_block = lax.dynamic_slice_in_dim(up_w, offset, group_size, 1)
            partial_sum = lax.dot_general(gate_cols, gate_block, (((1,), (1,)), ((), ())), preferred_element_type=jnp.float32)
            partial_sum = partial_sum + lax.dot_general(up_cols, up_block, (((1,), (1,)), ((), ())), preferred_element_type=jnp.float32)
            rounded = lax.optimization_barrier(partial_sum.astype(jnp.bfloat16))
            return running_sum + rounded.astype(jnp.float32), None

        summed, _ = lax.scan(add_group, jnp.zeros((block_count * CAP, D), jnp.float32), offsets)
        back_list.append(summed.astype(jnp.bfloat16))
        gate_list.append(gate_part)
        up_list.append(up_part)
        down_list.append(down_part)

    slots_back = jnp.stack(back_list).reshape(flight, block_count, CAP, D).transpose(1, 0, 2, 3).reshape(block_count, flight * CAP, D)

    def return_block(block_item):
        block_ids, block_back, block_grads_in = block_item
        pickers = selectors(route_places(block_ids, flight), flight)
        return combine_back(pickers, block_back, block_grads_in)

    attn_grad = lax.map(return_block, (id_blocks, slots_back, grad_blocks))

    query_half = queries.reshape(block_count, SEQ_DEV, ACTIVE_HEADS, HEAD_DIM)
    key_half = keys.reshape(block_count, SEQ_DEV, ACTIVE_HEADS, HEAD_DIM)
    value_half = values.reshape(block_count, SEQ_DEV, ACTIVE_HEADS, HEAD_DIM)
    grad_half = attn_grad.reshape(block_count, SEQ_DEV, ACTIVE_HEADS, HEAD_DIM)
    decay_blocks = log_decay.reshape(ACTIVE_HEADS, block_count, SEQ_DEV).transpose(1, 0, 2)
    running_all = jnp.cumsum(decay_blocks, axis=2)
    totals = running_all[:, :, -1]

    def state_terms(block_item):
        running, block_total, key_rows, value_rows, query_rows, grad_rows = block_item
        return local_state(block_total, running, key_rows, value_rows), grad_state(running, query_rows, grad_rows)

    own_states, own_grads = lax.map(state_terms, (running_all, totals, key_half, value_half, query_half, grad_half))

    def carry_step(running_sum, block_item):
        block_total, term = block_item
        return jnp.exp(block_total)[:, None, None] * running_sum + term, running_sum

    empty = jnp.zeros((ACTIVE_HEADS, HEAD_DIM, HEAD_DIM), jnp.float32)
    _, states_in = lax.scan(carry_step, empty, (totals, own_states))
    _, states_grad = lax.scan(carry_step, empty, (totals, own_grads), reverse=True)
    states_in = states_in.astype(jnp.bfloat16)
    states_grad = states_grad.astype(jnp.bfloat16)

    def grad_block(block_item):
        decay, query_rows, key_rows, value_rows, grad_rows, state_in, state_grad = block_item
        running, block_total, weights = decay_tables(decay)
        return block_grads(weights, running, block_total, query_rows, key_rows, value_rows, grad_rows, state_in, state_grad)

    q_grad, k_grad, v_grad = lax.map(grad_block, (decay_blocks, query_half, key_half, value_half, grad_half, states_in, states_grad))
    query_grad = q_grad.reshape(SEQUENCE_LENGTH, D).astype(jnp.bfloat16)
    key_grad = k_grad.reshape(SEQUENCE_LENGTH, D).astype(jnp.bfloat16)
    value_grad = v_grad.reshape(SEQUENCE_LENGTH, D).astype(jnp.bfloat16)
    return query_grad, key_grad, value_grad, jnp.stack(gate_list), jnp.stack(up_list), jnp.stack(down_list)
```

```python
import jax
import jax.numpy as jnp
from jax import lax
from jax.experimental import pallas as pl
from jax.experimental.pallas import tpu as pltpu
from jax.sharding import PartitionSpec as P

MESH = pl.DeviceIdType.MESH
BF16 = jnp.bfloat16
F32 = jnp.float32

FLIGHT = 4
D = 6144
QUARTER = D // 4
HID = 256
HEADS = 12
HALF_HEADS = HEADS // 2
HD = 128
ROWS = 128
MAIN = 256
SLOTS = 288
REM = 768
WIDE = D + REM
CUT = WIDE // 2
SHARE = 4 * 768 + 384
SHARE_CUT = 1792
BIG = 56 * 1024 * 1024


def dot(a, b):
    return lax.dot_general(a, b, (((1,), (0,)), ((), ())), preferred_element_type=F32)


def dot_nt(a, b):
    return lax.dot_general(a, b, (((1,), (1,)), ((), ())), preferred_element_type=F32)


def dot_tn(a, b):
    return lax.dot_general(a, b, (((0,), (0,)), ((), ())), preferred_element_type=F32)


def iota(shape, dim):
    return lax.broadcasted_iota(jnp.int32, shape, dim)


def aligned(value, by):
    return pl.multiple_of(value, by)


class Place:
    def __init__(self):
        ctx = lax.axis_index("ctx")
        self.x = lax.axis_index("exp")
        self.ctx = ctx
        self.core = lax.rem(ctx, 2)
        self.z = lax.rem(lax.div(ctx, 2), 4)
        self.y = lax.div(ctx, 8)
        self.chip = self.y * 4 + self.z

    def at(self, y=None, z=None, core=None, x=None):
        y = self.y if y is None else y
        z = self.z if z is None else z
        core = self.core if core is None else core
        x = self.x if x is None else x
        return (y * 8 + z * 2 + core, x)

    def sibling(self):
        return self.at(core=1 - self.core)


class Wires:
    def __init__(self, place, send_sems, recv_sems):
        self.place, self.send_sems, self.recv_sems = place, send_sems, recv_sems
        self.names, self.sent = {}, []

    def slot(self, name):
        return self.names.setdefault(name, len(self.names))

    def send(self, name, src, dst, device):
        slot = self.slot(name)
        copy = pltpu.make_async_remote_copy(
            src_ref=src,
            dst_ref=dst,
            send_sem=self.send_sems.at[slot],
            recv_sem=self.recv_sems.at[slot],
            device_id=device,
            device_id_type=MESH,
        )
        copy.start()
        self.sent.append(copy)

    def arrived(self, name, region):
        slot = self.slot(name)
        pltpu.make_async_remote_copy(
            src_ref=region,
            dst_ref=region,
            send_sem=self.send_sems.at[slot],
            recv_sem=self.recv_sems.at[slot],
            device_id=self.place.sibling(),
            device_id_type=MESH,
        ).wait_recv()

    def drain(self):
        for copy in self.sent:
            copy.wait_send()
        self.sent = []


def greet(devices):
    barrier = pltpu.get_barrier_semaphore()
    for device in devices:
        pl.semaphore_signal(barrier, inc=1, device_id=device, device_id_type=MESH)
    pl.semaphore_wait(barrier, len(devices))


def route_masks(small, place):
    ids0, ids1 = small[16:17, :], small[17:18, :]
    gates0, gates1 = small[18:19, :], small[19:20, :]
    wanted = lax.broadcasted_iota(jnp.int32, (8, ROWS), 0).astype(F32)
    first = ids0 == wanted
    second = ids1 == wanted
    onehot = jnp.where(first | second, 1.0, 0.0)
    gates = jnp.where(first, gates0, 0.0) + jnp.where(second, gates1, 0.0)
    before = jnp.where(iota((ROWS, ROWS), 0) < iota((ROWS, ROWS), 1), 1.0, 0.0).astype(BF16)
    rank = dot(onehot.astype(BF16), before)
    rank = jnp.where(onehot > 0.5, rank, -1.0)

    def spread(a):
        return jnp.concatenate([jnp.broadcast_to(a[e : e + 1, :], (16, ROWS)) for e in range(FLIGHT)], axis=0)

    rank, gates = spread(rank), spread(gates)
    row = lax.rem(iota((64, ROWS), 0), 16)
    mine = lax.div(row, 8) == place.core
    slot = lax.rem(row, 8)
    main = jnp.where(mine & (rank == slot.astype(F32)), 1.0, 0.0)
    ninth = jnp.where(mine & (rank == 8.0), 1.0, 0.0)
    return main, ninth, slot, gates


def moe_kernel(
    small_ref, moe_ref, out_grad_ref, wg_hbm, wu_hbm, wd_hbm,
    x_out, g_out, hidden_out, gate_out, up_out, attn_out, decay_out,
    wg, wu, wd, rows, stage, staged, ninth_in, acc, gact, uact,
    part, theirs, fold, ring_a, ring_b, ring_m, ring_p, group, ring2_a, ring2_b, ring2_m, ring2_p,
    final, back, decay, send_sems, recv_sems, local_sems,
):
    here = Place()
    core, other = here.core, 1 - here.core
    wires = Wires(here, send_sems, recv_sems)

    loads = [
        pltpu.make_async_copy(wg_hbm, wg, local_sems.at[0]),
        pltpu.make_async_copy(wu_hbm, wu, local_sems.at[1]),
        pltpu.make_async_copy(wd_hbm, wd, local_sems.at[2]),
    ]
    for load in loads:
        load.start()

    turn = [lax.rem(here.x + d, 4) for d in range(4)]
    turn_y = [lax.rem(here.y + d, 4) for d in range(4)]
    turn_z = [lax.rem(here.z + d, 4) for d in range(4)]
    greet(
        [here.sibling()]
        + [here.at(x=turn[d]) for d in (1, 2, 3)]
        + [here.at(y=turn_y[d]) for d in (1, 2, 3)]
        + [here.at(z=turn_z[d]) for d in (1, 2, 3)]
    )

    small = small_ref[...]
    decay[here.ctx] = jnp.broadcast_to(jnp.sum(small[0:16, :], axis=1, keepdims=True), (16, ROWS))
    wires.send("d", decay.at[here.ctx], decay.at[here.ctx], here.sibling())

    main, ninth, slot, gates = route_masks(small, here)
    pick = main.astype(BF16)
    main_gate = jnp.sum(main * gates, axis=1, keepdims=True)
    ninth_gate = jnp.sum(ninth * gates, axis=1, keepdims=True)
    fold_at = lax.rem(here.x, 2) * 4
    picks = [
        jnp.where(slot == fold_at + b, ninth, 0.0).astype(BF16) for b in range(4)
    ]
    for which, source in enumerate((moe_ref, out_grad_ref)):
        chosen = dot(pick, source[...])
        extra = dot(picks[0], source[:, 0:384])
        for b in range(1, 4):
            extra = extra + dot(picks[b], source[:, 384 * b : 384 * (b + 1)])
        if which:
            chosen, extra = chosen * main_gate, extra * ninth_gate
        stage[which, :, 0:QUARTER] = chosen.astype(BF16)
        stage[which, :, QUARTER:] = extra.astype(BF16)
    wires.send("s", stage.at[other], staged, here.sibling())
    wires.arrived("s", staged)
    stage[core] = (stage[core].astype(F32) + staged[...].astype(F32)).astype(BF16)

    mine = rows.at[core]
    own_rows = pl.ds(aligned(here.chip * 16, 16), 16)
    for d in (1, 2, 3):
        to = pl.ds(aligned(turn[d] * 16, 16), 16)
        wires.send(
            ("x", d),
            stage.at[core, to, 0:QUARTER],
            mine.at[own_rows, pl.ds(aligned(here.x * QUARTER, QUARTER), QUARTER)],
            here.at(x=turn[d]),
        )
        wires.send(("xr", d), stage.at[core, to, QUARTER:], ninth_in.at[here.x], here.at(x=turn[d]))
    kept = pl.ds(aligned(here.x * 16, 16), 16)
    rows[core, own_rows, pl.ds(aligned(here.x * QUARTER, QUARTER), QUARTER)] = stage[core, kept, 0:QUARTER]
    ninth_in[here.x] = stage[core, kept, QUARTER:]

    wires.arrived("d", decay.at[here.at(core=other)[0]])
    pair = decay.at[pl.ds(here.chip * 2, 2)]
    for d in (1, 2, 3):
        wires.send(("dz", d), pair, pair, here.at(z=turn_z[d]))

    for d in (1, 2, 3):
        source = turn[4 - d]
        wires.arrived(("x", d), mine.at[own_rows, pl.ds(aligned(source * QUARTER, QUARTER), QUARTER)])
        wires.arrived(("xr", d), ninth_in.at[source])
    for p in range(2):
        rows[core, own_rows, D + 384 * p : D + 384 * (p + 1)] = (
            ninth_in[2 * p].astype(F32) + ninth_in[2 * p + 1].astype(F32)
        ).astype(BF16)

    first = jnp.where(core == 0, here.z, here.y)
    second = jnp.where(core == 0, here.y, here.z)
    first_step, second_step = jnp.where(core == 0, 1, 4), jnp.where(core == 0, 4, 1)
    fs = [lax.rem(first + d, 4) for d in range(4)]
    ss = [lax.rem(second + d, 4) for d in range(4)]

    def on_first(value):
        return here.at(y=jnp.where(core == 0, here.y, value), z=jnp.where(core == 0, value, here.z))

    def on_second(value):
        return here.at(y=jnp.where(core == 0, value, here.y), z=jnp.where(core == 0, here.z, value))

    left, right, full = pl.ds(0, CUT), pl.ds(CUT, CUT), pl.ds(0, WIDE)

    def tile(i, j, columns=full):
        at = (fs[i] * first_step + ss[j] * second_step) * 16
        return rows.at[core, pl.ds(aligned(at, 16), 16), columns]

    def their_tile(i, j):
        at = (ss[i] * second_step + fs[j] * first_step) * 16
        return rows.at[other, pl.ds(aligned(at, 16), 16), full]

    def share(i, j):
        wires.send(("c", i, j), tile(i, j), tile(i, j), here.sibling())

    def spread_second(i):
        wires.send(("s+", i), tile(i, 0), tile(i, 0), on_second(ss[1]))
        wires.send(("s-", i), tile(i, 0), tile(i, 0), on_second(ss[3]))
        share(i, 0)

    def pass_second(i):
        wires.arrived(("s+", i), tile(i, 3))
        wires.send(("s+l", i), tile(i, 3, left), tile(i, 3, left), on_second(ss[1]))
        share(i, 3)
        wires.arrived(("s-", i), tile(i, 1))
        wires.send(("s-r", i), tile(i, 1, right), tile(i, 1, right), on_second(ss[3]))
        share(i, 1)

    def end_second(i):
        wires.arrived(("s+l", i), tile(i, 2, left))
        wires.arrived(("s-r", i), tile(i, 2, right))
        share(i, 2)

    wires.send("f+", tile(0, 0), tile(0, 0), on_first(fs[1]))
    wires.send("f-", tile(0, 0), tile(0, 0), on_first(fs[3]))
    spread_second(0)
    wires.arrived("f+", tile(3, 0))
    wires.send("f+l", tile(3, 0, left), tile(3, 0, left), on_first(fs[1]))
    wires.arrived("f-", tile(1, 0))
    wires.send("f-r", tile(1, 0, right), tile(1, 0, right), on_first(fs[3]))
    spread_second(3)
    spread_second(1)
    pass_second(0)
    wires.arrived("f+l", tile(2, 0, left))
    wires.arrived("f-r", tile(2, 0, right))
    spread_second(2)
    for d in (1, 2, 3):
        source = turn_z[4 - d]
        wires.arrived(("dz", d), decay.at[pl.ds((here.y * 4 + source) * 2, 2)])
    line = decay.at[pl.ds(here.y * 8, 8)]
    for d in (1, 2, 3):
        wires.send(("dy", d), line, line, here.at(y=turn_y[d]))
    pass_second(3)
    pass_second(1)
    end_second(0)
    pass_second(2)
    end_second(3)
    end_second(1)
    end_second(2)
    for d in (1, 2, 3):
        wires.arrived(("dy", d), decay.at[pl.ds(turn_y[4 - d] * 8, 8)])
    decay_out[...] = decay[...]
    for i in range(4):
        for j in range(4):
            wires.arrived(("c", i, j), their_tile(i, j))

    r0, r1 = iota((MAIN, MAIN), 0), iota((MAIN, MAIN), 1)
    chip_core, grp = lax.rem(r0, 32), lax.div(r0, 32)
    unfold = jnp.where(r1 == chip_core * 8 + grp, 1.0, 0.0).astype(BF16)
    for which in range(2):
        for p in range(2):
            spread = dot(unfold, rows[which, 0:MAIN, D + 384 * p : D + 384 * (p + 1)]).astype(BF16)
            for g in range(8):
                at = (2 * p + g // 4) * QUARTER + (g % 4) * 384
                rows[which, MAIN:SLOTS, at : at + 384] = spread[32 * g : 32 * (g + 1), :]
    stores = [
        pltpu.make_async_copy(rows.at[0, :, 0:D], x_out, local_sems.at[3]),
        pltpu.make_async_copy(rows.at[1, :, 0:D], g_out, local_sems.at[4]),
    ]
    for store in stores:
        store.start()

    for load in loads:
        load.wait()
    acc[...] = jnp.zeros_like(acc)

    def contract(j, _):
        at = pl.ds(aligned(j * 512, 512), 512)
        inputs, grads = rows[0, :, at], rows[1, :, at]
        acc[0] += dot(inputs, wg[at, :])
        acc[1] += dot(inputs, wu[at, :])
        acc[2] += dot_nt(grads, wd[:, at])
        return 0

    lax.fori_loop(0, D // 512, contract, 0)
    gate_pre, up_pre, hidden_grad = acc[0], acc[1], acc[2]
    sig = jax.nn.sigmoid(gate_pre)
    active = gate_pre * sig
    hidden_out[...] = (active * up_pre).astype(BF16)
    gact[...] = (hidden_grad * up_pre * sig * (1.0 + gate_pre * (1.0 - sig))).astype(BF16)
    uact[...] = (hidden_grad * active).astype(BF16)
    gate_out[...] = gact[...]
    up_out[...] = uact[...]

    def slot_part(which, owner):
        y_step, z_step = jnp.where(owner == 0, 4, 1), jnp.where(owner == 0, 1, 4)

        def one(q, _):
            at = pl.ds(aligned(q * QUARTER + owner * 768, 768), 768)
            piece = dot_nt(gact[...], wg[at, :]) + dot_nt(uact[...], wu[at, :])
            piece = piece.astype(BF16)
            columns = pl.ds(aligned(q * 768, 768), 768)
            for k in range(16):
                to = ((k // 4) * y_step + (k % 4) * z_step) * 16
                part[which, pl.ds(aligned(to, 16), 16), columns] = piece[16 * k : 16 * (k + 1), :]
            for b in range(2):
                fold[pl.ds(aligned((q * 2 + b) * 32, 32), 32), :] = piece[MAIN:, 384 * b : 384 * (b + 1)]
            return 0

        lax.fori_loop(0, 4, one, 0)
        position, inside = lax.div(r0, 16), lax.rem(r0, 16)
        chip = jnp.where(owner == 0, position, lax.rem(position, 4) * 4 + lax.div(position, 4))
        source = lax.rem(inside, 8) * 32 + chip * 2 + lax.div(inside, 8)
        refold = jnp.where(r1 == source, 1.0, 0.0).astype(BF16)
        part[which, :, 3072:] = dot(refold, fold[...]).astype(BF16)

    slot_part(1, other)
    wires.send("p", part.at[1], theirs, here.sibling())
    slot_part(0, core)
    wires.arrived("p", theirs)

    def join(j, _):
        at = pl.ds(aligned(j * 16, 16), 16)
        part[0, at, :] = (part[0, at, :].astype(F32) + theirs[at, :].astype(F32)).astype(BF16)
        return 0

    lax.fori_loop(0, 16, join, 0)

    cl, cr = pl.ds(0, SHARE_CUT), pl.ds(SHARE_CUT, SHARE - SHARE_CUT)

    def ring_sum(tag, buffer, height, places, device, in_a, in_b, in_m, in_p, store_result):
        def block(i, columns):
            return buffer.at[pl.ds(aligned(places[i] * height, height), height), columns]

        def add_into(i, columns, arrived_ref):
            at = pl.ds(aligned(places[i] * height, height), height)
            buffer[at, columns] = (buffer[at, columns].astype(F32) + arrived_ref[...].astype(F32)).astype(BF16)

        up, down = device(places[1]), device(places[3])
        wires.send((tag, "a"), block(2, cl), in_a, up)
        wires.send((tag, "b"), block(2, cr), in_b, down)
        wires.send((tag, "mr"), block(1, cr), in_m.at[:, cr], up)
        wires.send((tag, "pl"), block(3, cl), in_p.at[:, cl], down)
        wires.arrived((tag, "a"), in_a)
        add_into(1, cl, in_a)
        wires.send((tag, "ml"), block(1, cl), in_m.at[:, cl], up)
        wires.arrived((tag, "b"), in_b)
        add_into(3, cr, in_b)
        wires.send((tag, "pr"), block(3, cr), in_p.at[:, cr], down)
        wires.arrived((tag, "mr"), in_m.at[:, cr])
        wires.arrived((tag, "pl"), in_p.at[:, cl])
        wires.arrived((tag, "ml"), in_m.at[:, cl])
        wires.arrived((tag, "pr"), in_p.at[:, cr])
        at = pl.ds(aligned(places[0] * height, height), height)
        store_result(
            (buffer[at, :].astype(F32) + in_m[...].astype(F32) + in_p[...].astype(F32)).astype(BF16)
        )

    def keep_group(value):
        group[...] = value

    def keep_final(value):
        final[...] = value

    ring_sum("r1", part.at[0], 64, ss, on_second, ring_a, ring_b, ring_m, ring_p, keep_group)
    ring_sum("r2", group, 16, fs, on_first, ring2_a, ring2_b, ring2_m, ring2_p, keep_final)

    own_back = pl.ds(aligned(here.x * 16, 16), 16)
    for d in (1, 2, 3):
        columns = pl.ds(aligned(turn[d] * 768, 768), 768)
        wires.send(("b", d), final.at[:, columns], back.at[core, own_back, 0:768], here.at(x=turn[d]))
        wires.send(("br", d), final.at[:, 3072:], back.at[core, own_back, 768:], here.at(x=turn[d]))
    back[core, own_back, 0:768] = final[:, pl.ds(aligned(here.x * 768, 768), 768)]
    back[core, own_back, 768:] = final[:, 3072:]
    for d in (1, 2, 3):
        source = pl.ds(aligned(turn[4 - d] * 16, 16), 16)
        wires.arrived(("b", d), back.at[core, source, 0:768])
        wires.arrived(("br", d), back.at[core, source, 768:])
    wires.send("bc", back.at[core], back.at[core], here.sibling())
    wires.arrived("bc", back.at[other])

    for b in range(2):
        chosen = jnp.where(slot == 2 * here.x + b, ninth, 0.0)
        pick_back = jnp.concatenate([main, chosen], axis=0).astype(BF16)
        for h in range(2):
            at = h * 768 + b * 384
            source = jnp.concatenate(
                [back[h, :, 384 * b : 384 * (b + 1)], back[h, :, 768:]], axis=0
            )
            attn_out[:, at : at + 384] = (
                out_grad_ref[:, at : at + 384].astype(F32) + dot_tn(pick_back, source)
            ).astype(BF16)

    for store in stores:
        store.wait()
    wires.drain()


def scan_kernel(
    small_ref, decay_ref, q_ref, k_ref, v_ref, g_ref,
    dq_out, dk_out, dv_out,
    states, sib, totals, z_in, y_in, results, r_in, for_sib, final, turned, kept, send_sems, recv_sems,
):
    here = Place()
    core, other = here.core, 1 - here.core
    wires = Wires(here, send_sems, recv_sems)
    turn_y = [lax.rem(here.y + d, 4) for d in range(4)]
    turn_z = [lax.rem(here.z + d, 4) for d in range(4)]
    greet(
        [here.sibling()]
        + [here.at(y=turn_y[d]) for d in (1, 2, 3)]
        + [here.at(z=turn_z[d]) for d in (1, 2, 3)]
    )

    run = small_ref[0:16, :]
    lane = iota((16, ROWS), 1)
    step = 1
    while step < ROWS:
        run = run + jnp.where(lane >= step, pltpu.roll(run, step, 1), 0.0)
        step *= 2
    turned[...] = jnp.concatenate([run, jnp.zeros((ROWS - 16, ROWS), F32)], axis=0).T
    total = run[:, ROWS - 1 :]

    def head(h):
        at = slice(h * HD, (h + 1) * HD)
        return q_ref[:, at], k_ref[:, at], v_ref[:, at], g_ref[:, at]

    def columns(h):
        front = turned[:, h : h + 1]
        return jnp.exp(front), jnp.exp(total[h : h + 1, :] - front)

    for h in range(HEADS):
        q, k, v, g = head(h)
        front, tail = columns(h)
        decayed_k = (tail * k.astype(F32)).astype(BF16)
        decayed_q = (front * q.astype(F32)).astype(BF16)
        states[0, h] = dot_tn(decayed_k, v).astype(BF16).reshape(4, 32, HD)
        states[1, h] = dot_tn(decayed_q, g).astype(BF16).reshape(4, 32, HD)
    wires.send("s", states.at[:, pl.ds(other * HALF_HEADS, HALF_HEADS)], sib, here.sibling())

    lower = iota((ROWS, ROWS), 0) >= iota((ROWS, ROWS), 1)

    def local(h):
        q, k, v, g = head(h)
        spread = turned[:, h : h + 1] - run[h : h + 1, :]
        w = jnp.where(lower, jnp.exp(jnp.where(lower, spread, 0.0)), 0.0)
        mixed = (dot_nt(g, v) * w).astype(BF16)
        scores = (dot_nt(q, k) * w).astype(BF16)
        kept[0, h] = dot(mixed, k)
        kept[1, h] = dot_tn(mixed, q)
        kept[2, h] = dot_tn(scores, g)

    def log_total(block, h):
        return decay_ref[block, pl.ds(h, 1), :]

    wires.arrived("s", sib)
    even, odd = here.chip * 2, here.chip * 2 + 1
    for i in range(HALF_HEADS):
        hd = core * HALF_HEADS + i
        for way in range(2):
            own, far = states[way, hd].astype(F32), sib[way, i].astype(F32)
            s_even, s_odd = jnp.where(core == 0, own, far), jnp.where(core == 0, far, own)
            if way == 0:
                whole = s_odd + jnp.exp(log_total(odd, hd)) * s_even
            else:
                whole = s_even + jnp.exp(log_total(even, hd)) * s_odd
            whole = whole.astype(BF16)
            for quarter in range(4):
                totals[quarter, way, i] = whole[quarter]
    for d in (1, 2, 3):
        wires.send(("z", d), totals.at[turn_z[d]], z_in.at[here.z], here.at(z=turn_z[d]))
    z_in[here.z] = totals[here.z]
    for h in range(0, 6):
        local(h)
    for d in (1, 2, 3):
        wires.arrived(("z", d), z_in.at[turn_z[4 - d]])

    def chip_decay(y, z, hd):
        chip = (y * 4 + z) * 2
        return log_total(chip, hd) + log_total(chip + 1, hd)

    for i in range(HALF_HEADS):
        hd = core * HALF_HEADS + i
        for way in range(2):
            order = range(4) if way == 0 else range(3, -1, -1)
            acc = jnp.zeros((32, HD), F32)
            for z in order:
                acc = z_in[z, way, i].astype(F32) + jnp.exp(chip_decay(here.y, z, hd)) * acc
            y_in[here.y, way, i] = acc.astype(BF16)
    for d in (1, 2, 3):
        wires.send(("y", d), y_in.at[here.y], y_in.at[here.y], here.at(y=turn_y[d]))
    for h in range(6, HEADS):
        local(h)
    for d in (1, 2, 3):
        wires.arrived(("y", d), y_in.at[turn_y[4 - d]])

    for i in range(HALF_HEADS):
        hd = core * HALF_HEADS + i
        for way in range(2):
            acc = jnp.zeros((32, HD), F32)
            for y in (0, 1, 2) if way == 0 else (3, 2, 1):
                line = chip_decay(y, 0, hd)
                for z in (1, 2, 3):
                    line = line + chip_decay(y, z, hd)
                ahead = y < here.y if way == 0 else y > here.y
                acc = jnp.where(ahead, y_in[y, way, i].astype(F32) + jnp.exp(line) * acc, acc)
            order = range(4) if way == 0 else range(3, -1, -1)
            for z in order:
                results[z, way, i] = acc.astype(BF16)
                acc = z_in[z, way, i].astype(F32) + jnp.exp(chip_decay(here.y, z, hd)) * acc
    for d in (1, 2, 3):
        wires.send(("r", d), results.at[turn_z[d]], r_in.at[here.z], here.at(z=turn_z[d]))
    r_in[here.z] = results[here.z]
    for d in (1, 2, 3):
        wires.arrived(("r", d), r_in.at[turn_z[4 - d]])

    for i in range(HALF_HEADS):
        hd = core * HALF_HEADS + i
        for way in range(2):
            own, far = states[way, hd].astype(F32), sib[way, i].astype(F32)
            s_even, s_odd = jnp.where(core == 0, own, far), jnp.where(core == 0, far, own)
            enters = jnp.stack([r_in[quarter, way, i] for quarter in range(4)], axis=0).astype(F32)
            if way == 0:
                at_even = enters
                at_odd = s_even + jnp.exp(log_total(even, hd)) * enters
            else:
                at_odd = enters
                at_even = s_odd + jnp.exp(log_total(odd, hd)) * enters
            final[way, hd] = jnp.where(core == 0, at_even, at_odd).astype(BF16)
            for_sib[way, i] = jnp.where(core == 0, at_odd, at_even).astype(BF16)
    own_heads = pl.ds(core * HALF_HEADS, HALF_HEADS)
    wires.send("f", for_sib, final.at[:, own_heads], here.sibling())
    wires.arrived("f", final.at[:, pl.ds(other * HALF_HEADS, HALF_HEADS)])

    for h in range(HEADS):
        _, k, v, g = head(h)
        front, tail = columns(h)
        state_in, state_grad = final[0, h].reshape(HD, HD), final[1, h].reshape(HD, HD)
        at = slice(h * HD, (h + 1) * HD)
        dq_out[:, at] = (kept[0, h] + front * dot_nt(g, state_in)).astype(BF16)
        dk_out[:, at] = (kept[1, h] + tail * dot_nt(v, state_grad)).astype(BF16)
        dv_out[:, at] = (kept[2, h] + tail * dot(k, state_grad)).astype(BF16)
    wires.drain()


def in_vmem(count):
    return [pl.BlockSpec(memory_space=pltpu.VMEM)] * count


def in_hbm(count):
    return [pl.BlockSpec(memory_space=pl.ANY)] * count


def shape(dims, kind=BF16):
    return jax.ShapeDtypeStruct(dims, kind)


def moe_call(small, moe_input, out_grad, w_gate, w_up, w_down):
    sems = 80
    return pl.pallas_call(
        moe_kernel,
        out_shape=(
            shape((SLOTS, D)),
            shape((SLOTS, D)),
            shape((SLOTS, HID)),
            shape((SLOTS, HID)),
            shape((SLOTS, HID)),
            shape((ROWS, QUARTER)),
            shape((32, 16, ROWS), F32),
        ),
        in_specs=in_vmem(3) + in_hbm(3),
        out_specs=tuple(in_hbm(2) + in_vmem(5)),
        scratch_shapes=[
            pltpu.VMEM((D, HID), BF16),
            pltpu.VMEM((D, HID), BF16),
            pltpu.VMEM((HID, D), BF16),
            pltpu.VMEM((2, SLOTS, WIDE), BF16),
            pltpu.VMEM((2, 64, QUARTER + 384), BF16),
            pltpu.VMEM((64, QUARTER + 384), BF16),
            pltpu.VMEM((4, 16, 384), BF16),
            pltpu.VMEM((3, SLOTS, HID), F32),
            pltpu.VMEM((SLOTS, HID), BF16),
            pltpu.VMEM((SLOTS, HID), BF16),
            pltpu.VMEM((2, MAIN, SHARE), BF16),
            pltpu.VMEM((MAIN, SHARE), BF16),
            pltpu.VMEM((MAIN, 384), BF16),
            pltpu.VMEM((64, SHARE_CUT), BF16),
            pltpu.VMEM((64, SHARE - SHARE_CUT), BF16),
            pltpu.VMEM((64, SHARE), BF16),
            pltpu.VMEM((64, SHARE), BF16),
            pltpu.VMEM((64, SHARE), BF16),
            pltpu.VMEM((16, SHARE_CUT), BF16),
            pltpu.VMEM((16, SHARE - SHARE_CUT), BF16),
            pltpu.VMEM((16, SHARE), BF16),
            pltpu.VMEM((16, SHARE), BF16),
            pltpu.VMEM((16, SHARE), BF16),
            pltpu.VMEM((2, 64, 1152), BF16),
            pltpu.VMEM((32, 16, ROWS), F32),
            pltpu.SemaphoreType.DMA((sems,)),
            pltpu.SemaphoreType.DMA((sems,)),
            pltpu.SemaphoreType.DMA((5,)),
        ],
        compiler_params=pltpu.CompilerParams(
            collective_id=0, has_side_effects=True, vmem_limit_bytes=BIG
        ),
        name="routed_experts",
    )(small, moe_input, out_grad, w_gate, w_up, w_down)


def scan_call(small, decay, queries, keys, values, attn_grad):
    sems = 16
    half = (HALF_HEADS, 4, 32, HD)
    piece = (4, 2, HALF_HEADS, 32, HD)
    return pl.pallas_call(
        scan_kernel,
        out_shape=(shape((ROWS, QUARTER)),) * 3,
        in_specs=in_vmem(6),
        out_specs=tuple(in_vmem(3)),
        scratch_shapes=[
            pltpu.VMEM((2, HEADS, 4, 32, HD), BF16),
            pltpu.VMEM((2,) + half, BF16),
            pltpu.VMEM(piece, BF16),
            pltpu.VMEM(piece, BF16),
            pltpu.VMEM(piece, BF16),
            pltpu.VMEM(piece, BF16),
            pltpu.VMEM(piece, BF16),
            pltpu.VMEM((2,) + half, BF16),
            pltpu.VMEM((2, HEADS, 4, 32, HD), BF16),
            pltpu.VMEM((ROWS, ROWS), F32),
            pltpu.VMEM((3, HEADS, ROWS, HD), F32),
            pltpu.SemaphoreType.DMA((sems,)),
            pltpu.SemaphoreType.DMA((sems,)),
        ],
        compiler_params=pltpu.CompilerParams(
            collective_id=1, has_side_effects=True, vmem_limit_bytes=BIG
        ),
        name="state_scans",
    )(small, decay, queries, keys, values, attn_grad)


def on_device(
    queries, keys, values, log_decay, moe_input, out_grad, expert_ids, route_gates, w_gate, w_up, w_down
):
    small = jnp.concatenate(
        [
            jnp.pad(log_decay, ((0, 4), (0, 0))),
            expert_ids.T.astype(F32),
            route_gates.T,
            jnp.zeros((4, ROWS), F32),
        ],
        axis=0,
    )
    inputs, grads, hidden, gate_act, up_act, attn_grad, decay = moe_call(
        small, moe_input, out_grad, w_gate[0], w_up[0], w_down[0]
    )
    query_grad, key_grad, value_grad = scan_call(small, decay, queries, keys, values, attn_grad)
    gate_part = dot_tn(inputs, gate_act).astype(BF16)
    up_part = dot_tn(inputs, up_act).astype(BF16)
    down_part = dot_tn(hidden, grads).astype(BF16)
    return (query_grad, key_grad, value_grad, gate_part[None], up_part[None], down_part[None])


def solution(mesh):
    rows, heads = P("ctx", "exp"), P("exp", "ctx")
    columns, down = P("exp", None, "ctx"), P("exp", "ctx", None)
    return jax.shard_map(
        on_device,
        mesh=mesh,
        in_specs=(rows, rows, rows, heads, rows, rows, P("ctx", None), P("ctx", None), columns, columns, down),
        out_specs=(rows, rows, rows, columns, columns, down),
        check_vma=False,
    )
```

```python
import jax
import jax.numpy as jnp
from jax import lax
from jax.experimental import pallas as pl
from jax.experimental.pallas import tpu as pltpu
from jax.sharding import PartitionSpec as P

MESH = pl.DeviceIdType.MESH
BF16 = jnp.bfloat16
F32 = jnp.float32

FLIGHT = 4
D = 6144
QUARTER = D // 4
HID = 256
HEADS = 12
HALF_HEADS = HEADS // 2
HD = 128
ROWS = 128
MAIN = 256
SLOTS = 288
PAIR = 2 * QUARTER + 384
PAIR_CUT = 1792
WIDE = 2 * PAIR
CHUNKS = (1536, 1920)
CHUNK_CUTS = (768, 1024)
SENDS = 91
RECEIVES = 133
BIG = 42 * 1024 * 1024


def dot(a, b):
    return lax.dot_general(a, b, (((1,), (0,)), ((), ())), preferred_element_type=F32)


def dot_nt(a, b):
    return lax.dot_general(a, b, (((1,), (1,)), ((), ())), preferred_element_type=F32)


def dot_tn(a, b):
    return lax.dot_general(a, b, (((0,), (0,)), ((), ())), preferred_element_type=F32)


def iota(shape, dim):
    return lax.broadcasted_iota(jnp.int32, shape, dim)


def aligned(value, by):
    return pl.multiple_of(value, by)


class Place:
    def __init__(self):
        ctx = lax.axis_index("ctx")
        self.x = lax.axis_index("exp")
        self.ctx = ctx
        self.core = lax.rem(ctx, 2)
        self.z = lax.rem(lax.div(ctx, 2), 4)
        self.y = lax.div(ctx, 8)
        self.chip = self.y * 4 + self.z

    def at(self, y=None, z=None, core=None, x=None):
        y = self.y if y is None else y
        z = self.z if z is None else z
        core = self.core if core is None else core
        x = self.x if x is None else x
        return (y * 8 + z * 2 + core, x)

    def sibling(self):
        return self.at(core=1 - self.core)


class Wires:
    def __init__(self, place, send_sems, recv_sems):
        self.place, self.send_sems, self.recv_sems = place, send_sems, recv_sems
        self.names, self.sent, self.most = {}, [], 0

    def slot(self, name):
        return self.names.setdefault(name, len(self.names))

    def send(self, name, src, dst, device):
        copy = pltpu.make_async_remote_copy(
            src_ref=src,
            dst_ref=dst,
            send_sem=self.send_sems.at[len(self.sent)],
            recv_sem=self.recv_sems.at[self.slot(name)],
            device_id=device,
            device_id_type=MESH,
        )
        copy.start()
        self.sent.append(copy)
        self.most = max(self.most, len(self.sent))

    def arrived(self, name, region):
        pltpu.make_async_remote_copy(
            src_ref=region,
            dst_ref=region,
            send_sem=self.send_sems.at[0],
            recv_sem=self.recv_sems.at[self.slot(name)],
            device_id=self.place.sibling(),
            device_id_type=MESH,
        ).wait_recv()

    def drain(self):
        for copy in self.sent:
            copy.wait_send()
        self.sent = []

    def check(self):
        assert self.most == SENDS and len(self.names) == RECEIVES, (self.most, len(self.names))


def greet(devices):
    for device in devices:
        pl.semaphore_signal(pltpu.get_barrier_semaphore(), inc=1, device_id=device, device_id_type=MESH)


def greeted(count):
    pl.semaphore_wait(pltpu.get_barrier_semaphore(), count)


def route_masks(ids, route_gates, place):
    wanted = iota((8, ROWS), 0)
    first = ids[0:1, :] == wanted
    second = ids[1:2, :] == wanted
    onehot = jnp.where(first | second, 1.0, 0.0)
    gates = jnp.where(first, route_gates[0:1, :], 0.0) + jnp.where(second, route_gates[1:2, :], 0.0)
    before = jnp.where(iota((ROWS, ROWS), 0) < iota((ROWS, ROWS), 1), 1.0, 0.0).astype(BF16)
    rank = dot(onehot.astype(BF16), before)
    rank = jnp.where(onehot > 0.5, rank, -1.0)

    def spread(a):
        return jnp.concatenate([jnp.broadcast_to(a[e : e + 1, :], (16, ROWS)) for e in range(FLIGHT)], axis=0)

    rank, gates = spread(rank), spread(gates)
    row = lax.rem(iota((64, ROWS), 0), 16)
    mine = lax.div(row, 8) == place.core
    slot = lax.rem(row, 8)
    main = jnp.where(mine & (rank == slot.astype(F32)), 1.0, 0.0)
    ninth = jnp.where(mine & (rank == 8.0), 1.0, 0.0)
    return main, ninth, slot, gates


def main_kernel(
    ids_hbm, route_gates_hbm, log_decay_hbm, moe_hbm, out_grad_hbm, q_hbm, k_hbm, v_hbm, wg_hbm, wu_hbm, wd_hbm,
    gate_out, up_out, down_out, dq, kept, state_out, tails,
    ids_ref, route_gates_ref, log_decay_ref,
    moe_ref, out_grad_ref, q_ref, k_ref, v_ref, wg, wu, wd, rows, stage, staged, ninth_in, acc, hidden, acts,
    part0, part1, theirs0, theirs1, fold,
    a0, b0, m0, p0, group0, landing0, a1, b1, m1, p1, group1, landing1,
    final0, final1, outgoing, back, decay, run, turned, scaled, attn,
    states, sib, totals, z_in, y_in, results, r_in, for_sib, final,
    send_sems, recv_sems, local_sems,
):
    here = Place()
    core, other = here.core, 1 - here.core
    wires = Wires(here, send_sems, recv_sems)
    def local_copy(src, dst, index):
        copy = pltpu.make_async_copy(src, dst, local_sems.at[index])
        copy.start()
        return copy

    across = [here.x, here.x + 1 - 2 * lax.rem(here.x, 2), lax.rem(here.x + 2, 4), 3 - here.x]
    turn_y = [lax.rem(here.y + d, 4) for d in range(4)]
    turn_z = [lax.rem(here.z + d, 4) for d in range(4)]
    greet(
        [here.sibling()]
        + [here.at(x=across[d]) for d in (1, 2, 3)]
        + [here.at(y=turn_y[d]) for d in (1, 2, 3)]
        + [here.at(z=turn_z[d]) for d in (1, 2, 3)]
    )
    tiny = [
        local_copy(log_decay_hbm, log_decay_ref, 0),
        local_copy(ids_hbm, ids_ref, 1),
        local_copy(route_gates_hbm, route_gates_ref, 2),
    ]
    early = [local_copy(moe_hbm, moe_ref, 3), local_copy(out_grad_hbm, out_grad_ref, 4)]
    soon = [local_copy(k_hbm, k_ref, 5), local_copy(q_hbm, q_ref, 6), local_copy(v_hbm, v_ref, 7)]
    loads = [local_copy(wg_hbm, wg, 8), local_copy(wu_hbm, wu, 9), local_copy(wd_hbm, wd, 10)]
    for load in tiny:
        load.wait()

    run[...] = jnp.zeros_like(run)
    run[0:HEADS, :] = log_decay_ref[...]
    log_decay = run[...]
    decay[here.ctx] = jnp.broadcast_to(jnp.sum(log_decay, axis=1, keepdims=True), (16, ROWS))

    main, ninth, slot, gates = route_masks(ids_ref[...], route_gates_ref[...], here)
    pick = main.astype(BF16)
    main_gate = jnp.sum(main * gates, axis=1, keepdims=True)
    ninth_gate = jnp.sum(ninth * gates, axis=1, keepdims=True)
    fold_at = lax.rem(here.x, 2) * 4
    for load in early:
        load.wait()
    picks = [jnp.where(slot == fold_at + b, ninth, 0.0).astype(BF16) for b in range(4)]
    for which, source in enumerate((moe_ref, out_grad_ref)):
        chosen = dot(pick, source[...])
        extra = dot(picks[0], source[:, 0:384])
        for b in range(1, 4):
            extra = extra + dot(picks[b], source[:, 384 * b : 384 * (b + 1)])
        if which:
            chosen, extra = chosen * main_gate, extra * ninth_gate
        stage[which, :, 0:QUARTER] = chosen.astype(BF16)
        stage[which, :, QUARTER:] = extra.astype(BF16)
    greeted(10)
    wires.send("s", stage.at[other], staged, here.sibling())
    wires.send("d", decay.at[here.ctx], decay.at[here.ctx], here.sibling())

    lane = iota((16, ROWS), 1)
    step = 1
    while step < ROWS:
        log_decay = log_decay + jnp.where(lane >= step, pltpu.roll(log_decay, step, 1), 0.0)
        step *= 2
    run[...] = log_decay
    turned[...] = jnp.concatenate([log_decay, jnp.zeros((ROWS - 16, ROWS), F32)], axis=0).T
    ends = jnp.concatenate(
        [jnp.broadcast_to(log_decay[:, ROWS - 1 :], (16, ROWS)), jnp.zeros((ROWS - 16, ROWS), F32)], axis=0
    ).T
    tails[...] = jnp.exp(ends - turned[...])

    wires.arrived("s", staged)
    stage[core] = (stage[core].astype(F32) + staged[...].astype(F32)).astype(BF16)

    mine = rows.at[core]
    own_rows = pl.ds(aligned(here.chip * 16, 16), 16)

    def quarter_at(x):
        return pl.ds(aligned(lax.div(x, 2) * PAIR + lax.rem(x, 2) * QUARTER, 128), QUARTER)

    for d in (1, 2, 3):
        to = pl.ds(aligned(across[d] * 16, 16), 16)
        wires.send(
            ("x", d), stage.at[core, to, 0:QUARTER], mine.at[own_rows, quarter_at(here.x)], here.at(x=across[d])
        )
        wires.send(("xr", d), stage.at[core, to, QUARTER:], ninth_in.at[here.x], here.at(x=across[d]))
    to = pl.ds(aligned(here.x * 16, 16), 16)
    rows[core, own_rows, quarter_at(here.x)] = stage[core, to, 0:QUARTER]
    ninth_in[here.x] = stage[core, to, QUARTER:]

    wires.arrived("d", decay.at[here.at(core=other)[0]])
    pair_of_blocks = decay.at[pl.ds(here.chip * 2, 2)]
    for d in (1, 2, 3):
        wires.send(("dz", d), pair_of_blocks, pair_of_blocks, here.at(z=turn_z[d]))

    def log_total(block, h):
        return decay[block, pl.ds(h, 1), :]

    def chip_decay(y, z, h):
        chip = (y * 4 + z) * 2
        return log_total(chip, h) + log_total(chip + 1, h)

    even, odd = here.chip * 2, here.chip * 2 + 1

    def scan(way, source):
        heads = [core * HALF_HEADS + i for i in range(HALF_HEADS)]
        order = range(4) if way == 0 else range(3, -1, -1)

        def own_states(half):
            for i in range(HALF_HEADS):
                h = half * HALF_HEADS + i
                at = pl.ds(aligned(h * HD, HD), HD)
                states[way, h] = dot_tn(scaled[way, :, at], source[:, at]).astype(BF16).reshape(4, 32, HD)

        def both_states(i):
            own, far = states[way, heads[i]].astype(F32), sib[way, i].astype(F32)
            return jnp.where(core == 0, own, far), jnp.where(core == 0, far, own)

        own_states(other)
        wires.send(("s", way), states.at[way, pl.ds(other * HALF_HEADS, HALF_HEADS)], sib.at[way], here.sibling())
        own_states(core)
        yield
        wires.arrived(("s", way), sib.at[way])
        for i, h in enumerate(heads):
            s_even, s_odd = both_states(i)
            if way == 0:
                whole = s_odd + jnp.exp(log_total(odd, h)) * s_even
            else:
                whole = s_even + jnp.exp(log_total(even, h)) * s_odd
            whole = whole.astype(BF16)
            for quarter in range(4):
                totals[way, quarter, i] = whole[quarter]
        for d in (1, 2, 3):
            wires.send(("z", way, d), totals.at[way, turn_z[d]], z_in.at[way, here.z], here.at(z=turn_z[d]))
        z_in[way, here.z] = totals[way, here.z]
        yield
        for d in (1, 2, 3):
            wires.arrived(("z", way, d), z_in.at[way, turn_z[4 - d]])
        for i, h in enumerate(heads):
            total = jnp.zeros((32, HD), F32)
            for z in order:
                total = z_in[way, z, i].astype(F32) + jnp.exp(chip_decay(here.y, z, h)) * total
            y_in[way, here.y, i] = total.astype(BF16)
        for d in (1, 2, 3):
            wires.send(("y", way, d), y_in.at[way, here.y], y_in.at[way, here.y], here.at(y=turn_y[d]))
        yield
        for d in (1, 2, 3):
            wires.arrived(("y", way, d), y_in.at[way, turn_y[4 - d]])
        for i, h in enumerate(heads):
            total = jnp.zeros((32, HD), F32)
            for y in (0, 1, 2) if way == 0 else (3, 2, 1):
                line = chip_decay(y, 0, h)
                for z in (1, 2, 3):
                    line = line + chip_decay(y, z, h)
                ahead = y < here.y if way == 0 else y > here.y
                total = jnp.where(ahead, y_in[way, y, i].astype(F32) + jnp.exp(line) * total, total)
            for z in order:
                results[way, z, i] = total.astype(BF16)
                total = z_in[way, z, i].astype(F32) + jnp.exp(chip_decay(here.y, z, h)) * total
        for d in (1, 2, 3):
            wires.send(("r", way, d), results.at[way, turn_z[d]], r_in.at[way, here.z], here.at(z=turn_z[d]))
        r_in[way, here.z] = results[way, here.z]
        yield
        for d in (1, 2, 3):
            wires.arrived(("r", way, d), r_in.at[way, turn_z[4 - d]])
        for i, h in enumerate(heads):
            s_even, s_odd = both_states(i)
            enters = jnp.stack([r_in[way, quarter, i] for quarter in range(4)], axis=0).astype(F32)
            if way == 0:
                at_even, at_odd = enters, s_even + jnp.exp(log_total(even, h)) * enters
            else:
                at_even, at_odd = s_odd + jnp.exp(log_total(odd, h)) * enters, enters
            for_sib[way, i] = jnp.where(core == 0, at_odd, at_even).astype(BF16)
            final[way, h] = jnp.where(core == 0, at_even, at_odd).astype(BF16)
        wires.send(("f", way), for_sib.at[way], final.at[way, pl.ds(core * HALF_HEADS, HALF_HEADS)], here.sibling())
        yield
        wires.arrived(("f", way), final.at[way, pl.ds(other * HALF_HEADS, HALF_HEADS)])
        yield

    for load in soon:
        load.wait()
    for h in range(HEADS):
        at = slice(h * HD, (h + 1) * HD)
        scaled[0, :, at] = (tails[:, h : h + 1] * k_ref[:, at].astype(F32)).astype(BF16)
        scaled[1, :, at] = (jnp.exp(turned[:, h : h + 1]) * q_ref[:, at].astype(F32)).astype(BF16)
    earlier = scan(0, v_ref)
    next(earlier)

    first = jnp.where(core == 0, here.z, here.y)
    second = jnp.where(core == 0, here.y, here.z)
    first_step, second_step = jnp.where(core == 0, 1, 4), jnp.where(core == 0, 4, 1)
    fs = [lax.rem(first + d, 4) for d in range(4)]
    ss = [lax.rem(second + d, 4) for d in range(4)]

    def on_first(value):
        return here.at(y=jnp.where(core == 0, here.y, value), z=jnp.where(core == 0, value, here.z))

    def on_second(value):
        return here.at(y=jnp.where(core == 0, value, here.y), z=jnp.where(core == 0, here.z, value))

    own_pair = lax.div(here.x, 2)
    pairs = (own_pair, 1 - own_pair)

    def enter(turn):
        for d in ((1,), (2, 3))[turn]:
            wires.arrived(("x", d), mine.at[own_rows, quarter_at(across[d])])
            wires.arrived(("xr", d), ninth_in.at[across[d]])
        p = pairs[turn]
        rows[core, own_rows, pl.ds(aligned(p * PAIR + 2 * QUARTER, 128), 384)] = (
            ninth_in[2 * p].astype(F32) + ninth_in[2 * p + 1].astype(F32)
        ).astype(BF16)

    def gather(turn):
        base = pairs[turn] * PAIR
        full = pl.ds(aligned(base, 128), PAIR)
        left = pl.ds(aligned(base, 128), PAIR_CUT)
        right = pl.ds(aligned(base + PAIR_CUT, 128), PAIR - PAIR_CUT)

        def tile(i, j, columns=full):
            at = (fs[i] * first_step + ss[j] * second_step) * 16
            return rows.at[core, pl.ds(aligned(at, 16), 16), columns]

        def send(name, region, device):
            wires.send((turn,) + name, region, region, device)

        def arrived(name, region):
            wires.arrived((turn,) + name, region)

        def share(i, j):
            send(("c", i, j), tile(i, j), here.sibling())

        def spread_second(i):
            send(("s+", i), tile(i, 0), on_second(ss[1]))
            send(("s-", i), tile(i, 0), on_second(ss[3]))
            share(i, 0)

        def pass_second(i):
            arrived(("s+", i), tile(i, 3))
            send(("s+l", i), tile(i, 3, left), on_second(ss[1]))
            share(i, 3)
            arrived(("s-", i), tile(i, 1))
            send(("s-r", i), tile(i, 1, right), on_second(ss[3]))
            share(i, 1)

        def end_second(i):
            arrived(("s+l", i), tile(i, 2, left))
            arrived(("s-r", i), tile(i, 2, right))
            share(i, 2)

        for d in (1, 3, 2):
            send(("f", d), tile(0, 0), on_first(fs[d]))
        spread_second(0)
        yield
        arrived(("f", 1), tile(3, 0))
        spread_second(3)
        arrived(("f", 3), tile(1, 0))
        spread_second(1)
        yield
        pass_second(0)
        yield
        arrived(("f", 2), tile(2, 0))
        spread_second(2)
        yield
        pass_second(3)
        yield
        pass_second(1)
        yield
        pass_second(2)
        yield
        end_second(0)
        yield
        end_second(3)
        yield
        end_second(1)
        yield
        end_second(2)
        yield
        for i in range(4):
            for j in range(4):
                at = (ss[i] * second_step + fs[j] * first_step) * 16
                arrived(("c", i, j), rows.at[other, pl.ds(aligned(at, 16), 16), full])
        yield

    enter(0)
    pull0, pull1 = gather(0), gather(1)
    next(pull0)
    enter(1)
    next(pull1)
    next(earlier)
    next(pull0)
    next(pull0)
    next(pull1)
    next(pull1)
    next(pull0)
    next(pull1)
    for d in (1, 2, 3):
        wires.arrived(("dz", d), decay.at[pl.ds((here.y * 4 + turn_z[4 - d]) * 2, 2)])
    line_of_blocks = decay.at[pl.ds(here.y * 8, 8)]
    for d in (1, 2, 3):
        wires.send(("dy", d), line_of_blocks, line_of_blocks, here.at(y=turn_y[d]))
    next(pull0)
    next(pull0)
    next(pull1)
    next(pull1)
    next(pull0)
    next(pull1)
    next(pull0)
    next(pull0)
    next(pull0)
    next(pull0)
    next(pull1)
    next(pull0)

    r0, r1 = iota((MAIN, MAIN), 0), iota((MAIN, MAIN), 1)

    def unfold(turn):
        chip_core, grp = lax.rem(r0, 32), lax.div(r0, 32)
        select = jnp.where(r1 == chip_core * 8 + grp, 1.0, 0.0).astype(BF16)
        base = pairs[turn] * PAIR
        for which in range(2):
            spread = dot(select, rows[which, 0:MAIN, pl.ds(aligned(base + 2 * QUARTER, 128), 384)]).astype(BF16)
            for g in range(8):
                at = pl.ds(aligned(base + g * 384, 128), 384)
                rows[which, MAIN:SLOTS, at] = spread[32 * g : 32 * (g + 1), :]

    def contract(turn, start, stop):
        def one(j, _):
            at = pl.ds(aligned(pairs[turn] * PAIR + j * 512, 128), 512)
            to = pl.ds(aligned(pairs[turn] * 2 * QUARTER + j * 512, 512), 512)
            inputs, grads = rows[0, :, at], rows[1, :, at]
            acc[0] += dot(inputs, wg[to, :])
            acc[1] += dot(inputs, wu[to, :])
            acc[2] += dot_nt(grads, wd[:, to])
            return 0

        lax.fori_loop(start, stop, one, 0)

    def weight_grads(start, stop):
        for i in range(start, stop):
            at = slice(1024 * i + 384 * (i // 3), 1024 * (i + 1) + 384 * (i // 3))
            to = slice(1024 * i, 1024 * (i + 1))
            both = dot_tn(rows[0, :, at], acts[...])
            gate_out[to, :] = both[:, 0:HID].astype(BF16)
            up_out[to, :] = both[:, HID:].astype(BF16)
            down_out[:, to] = dot_tn(hidden[...], rows[1, :, at]).astype(BF16)

    for load in loads:
        load.wait()
    acc[...] = jnp.zeros_like(acc)
    unfold(0)
    contract(0, 0, 2)
    next(pull1)
    contract(0, 2, 4)
    next(pull1)
    contract(0, 4, 6)
    next(pull1)
    for d in (1, 2, 3):
        wires.arrived(("dy", d), decay.at[pl.ds(turn_y[4 - d] * 8, 8)])
    next(earlier)
    next(pull1)
    unfold(1)
    contract(1, 0, 6)
    wires.drain()
    gate_pre, up_pre, hidden_grad = acc[0], acc[1], acc[2]
    sig = jax.nn.sigmoid(gate_pre)
    active = gate_pre * sig
    hidden[...] = (active * up_pre).astype(BF16)
    acts[:, 0:HID] = (hidden_grad * up_pre * sig * (1.0 + gate_pre * (1.0 - sig))).astype(BF16)
    acts[:, HID:] = (hidden_grad * active).astype(BF16)

    parts, theirs = (part0, part1), (theirs0, theirs1)

    def slot_part(which, owner, chunk):
        y_step, z_step = jnp.where(owner == 0, 4, 1), jnp.where(owner == 0, 1, 4)
        part = parts[chunk]

        def one(j, _):
            q = 2 * chunk + j
            at = pl.ds(aligned(q * QUARTER + owner * 768, 768), 768)
            piece = dot_nt(acts[:, 0:HID], wg[at, :]) + dot_nt(acts[:, HID:], wu[at, :])
            piece = piece.astype(BF16)
            columns = pl.ds(aligned(j * 768, 768), 768)
            for k in range(16):
                to = ((k // 4) * y_step + (k % 4) * z_step) * 16
                part[which, pl.ds(aligned(to, 16), 16), columns] = piece[16 * k : 16 * (k + 1), :]
            for b in range(2):
                fold[which, pl.ds(aligned((q * 2 + b) * 32, 32), 32), :] = piece[MAIN:, 384 * b : 384 * (b + 1)]
            return 0

        lax.fori_loop(0, 2, one, 0)
        if chunk:
            position, inside = lax.div(r0, 16), lax.rem(r0, 16)
            chip = jnp.where(owner == 0, position, lax.rem(position, 4) * 4 + lax.div(position, 4))
            source = lax.rem(inside, 8) * 32 + chip * 2 + lax.div(inside, 8)
            refold = jnp.where(r1 == source, 1.0, 0.0).astype(BF16)
            part[which, :, 1536:] = dot(refold, fold[which]).astype(BF16)

    def join(chunk):
        wires.arrived(("p", chunk), theirs[chunk])
        part, far = parts[chunk], theirs[chunk]

        def one(j, _):
            at = pl.ds(aligned(j * 16, 16), 16)
            part[0, at, :] = (part[0, at, :].astype(F32) + far[at, :].astype(F32)).astype(BF16)
            return 0

        lax.fori_loop(0, 16, one, 0)

    def ring_sum(tag, buffer, height, cut, places, device, in_a, in_b, in_m, in_p, result):
        cl, cr = pl.ds(0, cut), pl.ds(cut, in_m.shape[1] - cut)

        def block(i, columns):
            return buffer.at[pl.ds(aligned(places[i] * height, height), height), columns]

        def add_into(i, columns, arrived_ref):
            at = pl.ds(aligned(places[i] * height, height), height)
            buffer[at, columns] = (buffer[at, columns].astype(F32) + arrived_ref[...].astype(F32)).astype(BF16)

        up, down = device(places[1]), device(places[3])
        wires.send((tag, "a"), block(2, cl), in_a, up)
        wires.send((tag, "b"), block(2, cr), in_b, down)
        wires.send((tag, "mr"), block(1, cr), in_m.at[:, cr], up)
        wires.send((tag, "pl"), block(3, cl), in_p.at[:, cl], down)
        yield
        wires.arrived((tag, "a"), in_a)
        add_into(1, cl, in_a)
        wires.send((tag, "ml"), block(1, cl), in_m.at[:, cl], up)
        wires.arrived((tag, "b"), in_b)
        add_into(3, cr, in_b)
        wires.send((tag, "pr"), block(3, cr), in_p.at[:, cr], down)
        yield
        wires.arrived((tag, "mr"), in_m.at[:, cr])
        wires.arrived((tag, "pl"), in_p.at[:, cl])
        wires.arrived((tag, "ml"), in_m.at[:, cl])
        wires.arrived((tag, "pr"), in_p.at[:, cr])
        at = pl.ds(aligned(places[0] * height, height), height)
        result[...] = (buffer[at, :].astype(F32) + in_m[...].astype(F32) + in_p[...].astype(F32)).astype(BF16)
        yield

    def direct_sum(tag, buffer, places, device, landing, result):
        def block(i):
            return pl.ds(aligned(places[i] * 16, 16), 16)

        for d in (2, 1, 3):
            wires.send((tag, d), buffer.at[block(d), :], landing.at[d], device(places[d]))
        yield
        total = buffer[block(0), :].astype(F32)
        for d in (1, 3, 2):
            wires.arrived((tag, d), landing.at[d])
            total = total + landing[d].astype(F32)
        result[...] = total.astype(BF16)
        yield

    far0 = ring_sum("r0", part0.at[0], 64, CHUNK_CUTS[0], ss, on_second, a0, b0, m0, p0, group0)
    far1 = ring_sum("r1", part1.at[0], 64, CHUNK_CUTS[1], ss, on_second, a1, b1, m1, p1, group1)
    near0 = direct_sum("n0", group0, fs, on_first, landing0, final0)
    near1 = direct_sum("n1", group1, fs, on_first, landing1, final1)
    slot_part(1, other, 0)
    wires.send(("p", 0), part0.at[1], theirs0, here.sibling())
    slot_part(0, core, 0)
    slot_part(1, other, 1)
    wires.send(("p", 1), part1.at[1], theirs1, here.sibling())
    join(0)
    next(far0)
    slot_part(0, core, 1)
    join(1)
    next(far1)
    next(far0)
    next(far1)
    next(far0)
    next(near0)
    next(far1)
    next(near1)
    next(near0)
    next(near1)

    own_back = pl.ds(aligned(here.x * 16, 16), 16)
    back_main = [final0.at[:, 0:768], final0.at[:, 768:1536], final1.at[:, 0:768], final1.at[:, 768:1536]]
    for q in range(4):
        outgoing[16 * q : 16 * (q + 1), :] = back_main[q][...]
    for d in (1, 2, 3):
        source = outgoing.at[pl.ds(aligned(across[d] * 16, 16), 16), :]
        wires.send(("b", d), source, back.at[core, own_back, 0:768], here.at(x=across[d]))
        wires.send(("br", d), final1.at[:, 1536:], back.at[core, own_back, 768:], here.at(x=across[d]))
    back[core, own_back, 0:768] = outgoing[own_back, :]
    back[core, own_back, 768:] = final1[:, 1536:]
    next(earlier)
    weight_grads(0, 2)
    for d in (1, 2, 3):
        source = pl.ds(aligned(across[d] * 16, 16), 16)
        wires.arrived(("b", d), back.at[core, source, 0:768])
        wires.arrived(("br", d), back.at[core, source, 768:])
    wires.send("bc", back.at[core], back.at[core], here.sibling())
    weight_grads(2, 3)
    wires.arrived("bc", back.at[other])

    for b in range(2):
        chosen = jnp.where(slot == 2 * here.x + b, ninth, 0.0)
        pick_back = jnp.concatenate([main, chosen], axis=0).astype(BF16)
        for h in range(2):
            at = h * 768 + b * 384
            source = jnp.concatenate([back[h, :, 384 * b : 384 * (b + 1)], back[h, :, 768:]], axis=0)
            attn[:, at : at + 384] = (
                out_grad_ref[:, at : at + 384].astype(F32) + dot_tn(pick_back, source)
            ).astype(BF16)

    later = scan(1, attn)
    next(later)
    next(earlier)
    next(later)
    next(earlier)

    lower = iota((ROWS, ROWS), 0) >= iota((ROWS, ROWS), 1)

    def within(h):
        at = slice(h * HD, (h + 1) * HD)
        q, k, v, g = q_ref[:, at], k_ref[:, at], v_ref[:, at], attn[:, at]
        front = turned[:, h : h + 1]
        spread = front - run[h : h + 1, :]
        w = jnp.where(lower, jnp.exp(jnp.where(lower, spread, 0.0)), 0.0)
        mixed = (dot_nt(g, v) * w).astype(BF16)
        scores = (dot_nt(q, k) * w).astype(BF16)
        state_in = final[0, h].reshape(HD, HD)
        dq[:, at] = (dot(mixed, k) + jnp.exp(front) * dot_nt(g, state_in)).astype(BF16)
        kept[0, :, at] = dot_tn(mixed, q)
        kept[1, :, at] = dot_tn(scores, g)

    for h in range(0, 6):
        within(h)
    next(later)
    for h in range(6, HEADS):
        within(h)
    next(later)
    weight_grads(3, 6)
    next(later)
    next(later)
    state_out[...] = final[1]
    wires.drain()
    wires.check()


def last_kernel(
    gate_ref, up_ref, down_ref, dq_ref, kept_ref, state_ref, tail_ref, k_hbm, v_hbm,
    gate_hbm, up_hbm, down_hbm, dq_out, dk_out, dv_out,
    k_ref, v_ref, dk_ref, dv_ref, sems,
):
    copies = []

    def start(src, dst):
        copy = pltpu.make_async_copy(src, dst, sems.at[len(copies)])
        copy.start()
        copies.append(copy)
        return copy

    loads = [start(k_hbm, k_ref), start(v_hbm, v_ref)]
    stores = [
        start(src, dst)
        for src, dst in ((gate_ref, gate_hbm), (up_ref, up_hbm), (down_ref, down_hbm), (dq_ref, dq_out))
    ]
    for load in loads:
        load.wait()
    for h in range(HEADS):
        at = slice(h * HD, (h + 1) * HD)
        tail, state = tail_ref[:, h : h + 1], state_ref[h].reshape(HD, HD)
        dk_ref[:, at] = (kept_ref[0, :, at] + tail * dot_nt(v_ref[:, at], state)).astype(BF16)
        dv_ref[:, at] = (kept_ref[1, :, at] + tail * dot(k_ref[:, at], state)).astype(BF16)
    stores += [start(dk_ref, dk_out), start(dv_ref, dv_out)]
    for store in stores:
        store.wait()


def in_vmem(count):
    return [pl.BlockSpec(memory_space=pltpu.VMEM)] * count


def in_hbm(count):
    return [pl.BlockSpec(memory_space=pl.ANY)] * count


def shape(dims, kind=BF16):
    return jax.ShapeDtypeStruct(dims, kind)


def main_call(ids, route_gates, log_decay, moe_input, out_grad, queries, keys, values, w_gate, w_up, w_down):
    half = (2, HALF_HEADS, 4, 32, HD)
    piece = (2, 4, HALF_HEADS, 32, HD)
    wide = (2, HEADS, 4, 32, HD)

    def ring(width, cut):
        return [(64, cut), (64, width - cut), (64, width), (64, width), (64, width), (4, 16, width)]

    bf16_scratch = (
        [(ROWS, QUARTER)] * 5
        + [(D, HID), (D, HID), (HID, D), (2, SLOTS, WIDE), (2, 64, QUARTER + 384), (64, QUARTER + 384), (4, 16, 384)],
        [(SLOTS, HID), (SLOTS, 2 * HID)]
        + [(2, MAIN, CHUNKS[0]), (2, MAIN, CHUNKS[1]), (MAIN, CHUNKS[0]), (MAIN, CHUNKS[1]), (2, MAIN, 384)]
        + ring(CHUNKS[0], CHUNK_CUTS[0])
        + ring(CHUNKS[1], CHUNK_CUTS[1])
        + [(16, CHUNKS[0]), (16, CHUNKS[1]), (64, 768), (2, 64, 1152)],
        [(2, ROWS, QUARTER), (ROWS, QUARTER), wide, half, piece, piece, piece, piece, piece, half, wide],
    )
    f32_scratch = (
        [(3, SLOTS, HID)],
        [(32, 16, ROWS), (16, ROWS), (ROWS, ROWS)],
        [],
    )
    scratch = [pltpu.VMEM((2, ROWS), jnp.int32), pltpu.VMEM((2, ROWS), F32), pltpu.VMEM((HEADS, ROWS), F32)]
    for narrow, broad in zip(bf16_scratch, f32_scratch):
        scratch += [pltpu.VMEM(dims, BF16) for dims in narrow]
        scratch += [pltpu.VMEM(dims, F32) for dims in broad]
    return pl.pallas_call(
        main_kernel,
        out_shape=(
            pltpu.VMEM((D, HID), BF16),
            pltpu.VMEM((D, HID), BF16),
            pltpu.VMEM((HID, D), BF16),
            pltpu.VMEM((ROWS, QUARTER), BF16),
            pltpu.VMEM((2, ROWS, QUARTER), F32),
            pltpu.VMEM((HEADS, 4, 32, HD), BF16),
            pltpu.VMEM((ROWS, ROWS), F32),
        ),
        in_specs=[pl.BlockSpec(memory_space=pltpu.HBM)] * 11,
        out_specs=tuple(in_vmem(7)),
        scratch_shapes=scratch
        + [
            pltpu.SemaphoreType.DMA((SENDS,)),
            pltpu.SemaphoreType.DMA((RECEIVES,)),
            pltpu.SemaphoreType.DMA((11,)),
        ],
        compiler_params=pltpu.CompilerParams(collective_id=0, has_side_effects=True, vmem_limit_bytes=BIG),
        name="routed_experts_and_scans",
    )(
        *(
            pltpu.with_memory_space_constraint(a, pltpu.HBM)
            for a in (
                ids, route_gates, log_decay, moe_input, out_grad, queries, keys, values, w_gate, w_up, w_down
            )
        )
    )


def last_call(gate_grad, up_grad, down_grad, dq, kept, state, tails, keys, values):
    held = (gate_grad, up_grad, down_grad, dq, kept, state, tails)
    outputs = [(D, HID), (D, HID), (HID, D), (ROWS, QUARTER), (ROWS, QUARTER), (ROWS, QUARTER)]
    return pl.pallas_call(
        last_kernel,
        out_shape=tuple(shape(dims) for dims in outputs),
        in_specs=in_vmem(7) + [pl.BlockSpec(memory_space=pltpu.HBM)] * 2,
        out_specs=tuple(in_hbm(len(outputs))),
        scratch_shapes=[pltpu.VMEM((ROWS, QUARTER), BF16)] * 4 + [pltpu.SemaphoreType.DMA((8,))],
        compiler_params=pltpu.CompilerParams(vmem_limit_bytes=16 * 1024 * 1024),
        name="outputs",
    )(*(pltpu.with_memory_space_constraint(a, pltpu.VMEM) for a in held), keys, values)


def on_device(
    queries, keys, values, log_decay, moe_input, out_grad, expert_ids, route_gates, w_gate, w_up, w_down
):
    held = main_call(
        expert_ids.T, route_gates.T, log_decay, moe_input, out_grad, queries, keys, values, w_gate[0], w_up[0], w_down[0]
    )
    gate_part, up_part, down_part, query_grad, key_grad, value_grad = last_call(*held, keys, values)
    return (query_grad, key_grad, value_grad, gate_part[None], up_part[None], down_part[None])


def solution(mesh):
    rows, heads = P("ctx", "exp"), P("exp", "ctx")
    columns, down = P("exp", None, "ctx"), P("exp", "ctx", None)
    return jax.shard_map(
        on_device,
        mesh=mesh,
        in_specs=(rows, rows, rows, heads, rows, rows, P("ctx", None), P("ctx", None), columns, columns, down),
        out_specs=(rows, rows, rows, columns, columns, down),
        check_vma=False,
    )
```

```python
import jax
import jax.numpy as jnp
from jax import lax
from jax.experimental import pallas as pl
from jax.experimental.pallas import tpu as pltpu
from jax.sharding import PartitionSpec as P

MESH = pl.DeviceIdType.MESH
BF16 = jnp.bfloat16
F32 = jnp.float32

FLIGHT = 4
D = 6144
QUARTER = D // 4
HID = 256
HEADS = 12
HALF_HEADS = HEADS // 2
HD = 128
ROWS = 128
MAIN = 256
SLOTS = 288
PAIR = 2 * QUARTER + 384
PAIR_CUT = 1792
WIDE = 2 * PAIR
QUARTERS = ((0,), (1, 2), (3,))
CHUNKS = (768, 1536, 1152)
CHUNK_CUTS = (384, 768, 640)
SENDS = 81
RECEIVES = 182
BIG = 42 * 1024 * 1024


def dot(a, b):
    return lax.dot_general(a, b, (((1,), (0,)), ((), ())), preferred_element_type=F32)


def dot_nt(a, b):
    return lax.dot_general(a, b, (((1,), (1,)), ((), ())), preferred_element_type=F32)


def dot_tn(a, b):
    return lax.dot_general(a, b, (((0,), (0,)), ((), ())), preferred_element_type=F32)


def iota(shape, dim):
    return lax.broadcasted_iota(jnp.int32, shape, dim)


def aligned(value, by):
    return pl.multiple_of(value, by)


class Place:
    def __init__(self):
        ctx = lax.axis_index("ctx")
        self.x = lax.axis_index("exp")
        self.ctx = ctx
        self.core = lax.rem(ctx, 2)
        self.z = lax.rem(lax.div(ctx, 2), 4)
        self.y = lax.div(ctx, 8)
        self.chip = self.y * 4 + self.z

    def at(self, y=None, z=None, core=None, x=None):
        y = self.y if y is None else y
        z = self.z if z is None else z
        core = self.core if core is None else core
        x = self.x if x is None else x
        return (y * 8 + z * 2 + core, x)

    def sibling(self):
        return self.at(core=1 - self.core)


class Wires:
    def __init__(self, place, send_sems, recv_sems):
        self.place, self.send_sems, self.recv_sems = place, send_sems, recv_sems
        self.names, self.sent, self.free, self.most = {}, [], [], 0

    def slot(self, name):
        return self.names.setdefault(name, len(self.names))

    def send(self, name, src, dst, device):
        if not self.free:
            self.free, self.most = [self.most], self.most + 1
        semaphore = self.free.pop()
        copy = pltpu.make_async_remote_copy(
            src_ref=src,
            dst_ref=dst,
            send_sem=self.send_sems.at[semaphore],
            recv_sem=self.recv_sems.at[self.slot(name)],
            device_id=device,
            device_id_type=MESH,
        )
        copy.start()
        self.sent.append((copy, semaphore))

    def arrived(self, name, region):
        pltpu.make_async_remote_copy(
            src_ref=region,
            dst_ref=region,
            send_sem=self.send_sems.at[0],
            recv_sem=self.recv_sems.at[self.slot(name)],
            device_id=self.place.sibling(),
            device_id_type=MESH,
        ).wait_recv()

    def drain(self, count=None):
        count = len(self.sent) if count is None else count
        for copy, semaphore in self.sent[:count]:
            copy.wait_send()
            self.free.append(semaphore)
        self.sent = self.sent[count:]

    def check(self):
        assert self.most == SENDS and len(self.names) == RECEIVES, (self.most, len(self.names))


def greet(devices):
    for device in devices:
        pl.semaphore_signal(pltpu.get_barrier_semaphore(), inc=1, device_id=device, device_id_type=MESH)


def greeted(count):
    pl.semaphore_wait(pltpu.get_barrier_semaphore(), count)


def route_masks(ids, route_gates, place):
    wanted = iota((8, ROWS), 0)
    first = ids[0:1, :] == wanted
    second = ids[1:2, :] == wanted
    onehot = jnp.where(first | second, 1.0, 0.0)
    gates = jnp.where(first, route_gates[0:1, :], 0.0) + jnp.where(second, route_gates[1:2, :], 0.0)
    before = jnp.where(iota((ROWS, ROWS), 0) < iota((ROWS, ROWS), 1), 1.0, 0.0).astype(BF16)
    rank = dot(onehot.astype(BF16), before)
    rank = jnp.where(onehot > 0.5, rank, -1.0)

    def spread(a):
        return jnp.concatenate([jnp.broadcast_to(a[e : e + 1, :], (16, ROWS)) for e in range(FLIGHT)], axis=0)

    rank, gates = spread(rank), spread(gates)
    row = lax.rem(iota((64, ROWS), 0), 16)
    mine = lax.div(row, 8) == place.core
    slot = lax.rem(row, 8)
    main = jnp.where(mine & (rank == slot.astype(F32)), 1.0, 0.0)
    ninth = jnp.where(mine & (rank == 8.0), 1.0, 0.0)
    return main, ninth, slot, gates


def main_kernel(
    ids_hbm, route_gates_hbm, log_decay_hbm, moe_hbm, out_grad_hbm, q_hbm, k_hbm, v_hbm, wg_hbm, wu_hbm, wd_hbm,
    gate_out, up_out, down_out, dq, kept, state_out, tails,
    ids_ref, route_gates_ref, log_decay_ref,
    moe_ref, out_grad_ref, q_ref, k_ref, v_ref, wgu, wd, rows, stage, staged, ninth_in, acc, acc_down, hidden, acts,
    fold,
    outgoing, back, decay, run, turned, scaled, attn,
    states, sib, totals, t_in, results, r_in, for_sib, final,
    *rest,
):
    send_sems, recv_sems, local_sems = rest[-3:]
    parts, theirs, in_as, in_bs, in_ms, in_ps, groups, landings, sums = (
        rest[i : len(rest) - 3 : 9] for i in range(9)
    )
    here = Place()
    core, other = here.core, 1 - here.core
    wires = Wires(here, send_sems, recv_sems)
    def local_copy(src, dst, index):
        copy = pltpu.make_async_copy(src, dst, local_sems.at[index])
        copy.start()
        return copy

    across = [here.x, here.x + 1 - 2 * lax.rem(here.x, 2), lax.rem(here.x + 2, 4), 3 - here.x]
    turn_y = [lax.rem(here.y + d, 4) for d in range(4)]
    turn_z = [lax.rem(here.z + d, 4) for d in range(4)]
    tiny = [
        local_copy(log_decay_hbm, log_decay_ref, 0),
        local_copy(ids_hbm, ids_ref, 1),
        local_copy(route_gates_hbm, route_gates_ref, 2),
    ]
    early = [local_copy(moe_hbm, moe_ref, 3), local_copy(out_grad_hbm, out_grad_ref, 4)]
    greet(
        [here.sibling()]
        + [here.at(x=across[d]) for d in (1, 2, 3)]
        + [here.at(y=turn_y[dy], z=turn_z[dz]) for dy in range(4) for dz in range(4) if dy or dz]
    )
    soon = [local_copy(k_hbm, k_ref, 5), local_copy(q_hbm, q_ref, 6), local_copy(v_hbm, v_ref, 7)]
    loads = [
        local_copy(wg_hbm, wgu.at[:, 0:HID], 8),
        local_copy(wu_hbm, wgu.at[:, HID:], 9),
        local_copy(wd_hbm, wd, 10),
    ]
    for load in tiny:
        load.wait()

    run[...] = jnp.zeros_like(run)
    run[0:HEADS, :] = log_decay_ref[...]
    log_decay = run[...]
    decay[here.ctx] = jnp.broadcast_to(jnp.sum(log_decay, axis=1, keepdims=True), (16, ROWS))

    main, ninth, slot, gates = route_masks(ids_ref[...], route_gates_ref[...], here)
    pick = main.astype(BF16)
    main_gate = jnp.sum(main * gates, axis=1, keepdims=True)
    ninth_gate = jnp.sum(ninth * gates, axis=1, keepdims=True)
    fold_at = lax.rem(here.x, 2) * 4
    for load in early:
        load.wait()
    picks = [jnp.where(slot == fold_at + b, ninth, 0.0).astype(BF16) for b in range(4)]
    for which, source in enumerate((moe_ref, out_grad_ref)):
        chosen = dot(pick, source[...])
        extra = dot(picks[0], source[:, 0:384])
        for b in range(1, 4):
            extra = extra + dot(picks[b], source[:, 384 * b : 384 * (b + 1)])
        if which:
            chosen, extra = chosen * main_gate, extra * ninth_gate
        stage[which, :, 0:QUARTER] = chosen.astype(BF16)
        stage[which, :, QUARTER:] = extra.astype(BF16)
    greeted(19)
    wires.send("s", stage.at[other], staged, here.sibling())
    wires.send("d", decay.at[here.ctx], decay.at[here.ctx], here.sibling())

    lane = iota((16, ROWS), 1)
    step = 1
    while step < ROWS:
        log_decay = log_decay + jnp.where(lane >= step, pltpu.roll(log_decay, step, 1), 0.0)
        step *= 2
    run[...] = log_decay
    turned[...] = jnp.concatenate([log_decay, jnp.zeros((ROWS - 16, ROWS), F32)], axis=0).T
    ends = jnp.concatenate(
        [jnp.broadcast_to(log_decay[:, ROWS - 1 :], (16, ROWS)), jnp.zeros((ROWS - 16, ROWS), F32)], axis=0
    ).T
    tails[...] = jnp.exp(ends - turned[...])

    wires.arrived("s", staged)
    stage[core] = (stage[core].astype(F32) + staged[...].astype(F32)).astype(BF16)

    mine = rows.at[core]
    own_rows = pl.ds(aligned(here.chip * 16, 16), 16)

    def quarter_at(x):
        return pl.ds(aligned(lax.div(x, 2) * PAIR + lax.rem(x, 2) * QUARTER, 128), QUARTER)

    def to_owner(d):
        to = pl.ds(aligned(across[d] * 16, 16), 16)
        wires.send(
            ("x", d), stage.at[core, to, 0:QUARTER], mine.at[own_rows, quarter_at(here.x)], here.at(x=across[d])
        )
        wires.send(("xr", d), stage.at[core, to, QUARTER:], ninth_in.at[here.x], here.at(x=across[d]))

    to_owner(1)
    to_owner(3)
    to = pl.ds(aligned(here.x * 16, 16), 16)
    rows[core, own_rows, quarter_at(here.x)] = stage[core, to, 0:QUARTER]
    ninth_in[here.x] = stage[core, to, QUARTER:]

    wires.arrived("d", decay.at[here.at(core=other)[0]])
    pair_of_blocks = decay.at[pl.ds(here.chip * 2, 2)]
    for d in (1, 2, 3):
        wires.send(("dz", d), pair_of_blocks, pair_of_blocks, here.at(z=turn_z[d]))

    def log_total(block, h):
        return decay[block, pl.ds(h, 1), :]

    even, odd = here.chip * 2, here.chip * 2 + 1

    apart = [(dy, dz) for dy in (2, 1, 3, 0) for dz in (2, 1, 3, 0) if dy or dz]

    def chip_at(dy, dz):
        return turn_y[dy % 4] * 4 + turn_z[dz % 4]

    def scan(way, source):
        heads = [core * HALF_HEADS + i for i in range(HALF_HEADS)]
        order = range(16) if way == 0 else range(15, -1, -1)

        def own_states(half):
            for i in range(HALF_HEADS):
                h = half * HALF_HEADS + i
                at = pl.ds(aligned(h * HD, HD), HD)
                states[way, h] = dot_tn(scaled[way, :, at], source[:, at]).astype(BF16).reshape(8, 16, HD)

        def both_states(i):
            own, far = states[way, heads[i]].astype(F32), sib[way, i].astype(F32)
            return jnp.where(core == 0, own, far), jnp.where(core == 0, far, own)

        own_states(other)
        wires.send(("s", way), states.at[way, pl.ds(other * HALF_HEADS, HALF_HEADS)], sib.at[way], here.sibling())
        own_states(core)
        yield
        wires.arrived(("s", way), sib.at[way])
        for i, h in enumerate(heads):
            s_even, s_odd = both_states(i)
            if way == 0:
                whole = s_odd + jnp.exp(log_total(odd, h)) * s_even
            else:
                whole = s_even + jnp.exp(log_total(even, h)) * s_odd
            whole = whole.astype(BF16)
            for piece in range(8):
                totals[way, 2 * piece + i // 3, i % 3] = whole[piece]
        for dy, dz in apart:
            wires.send(
                ("t", way, dy, dz),
                totals.at[way, chip_at(dy, dz)],
                t_in.at[way, here.chip],
                here.at(y=turn_y[dy], z=turn_z[dz]),
            )
        t_in[way, here.chip] = totals[way, here.chip]
        yield
        for dy, dz in reversed(apart):
            wires.arrived(("t", way, dy, dz), t_in.at[way, chip_at(-dy, -dz)])
        for i in range(3):
            h = core * HALF_HEADS + 3 * lax.rem(here.chip, 2) + i
            total = jnp.zeros((16, HD), F32)
            for n in order:
                results[way, n, i] = total.astype(BF16)
                decayed = jnp.exp(log_total(2 * n, h) + log_total(2 * n + 1, h))
                total = t_in[way, n, i].astype(F32) + decayed * total
        for dy, dz in apart:
            wires.send(
                ("r", way, dy, dz),
                results.at[way, chip_at(dy, dz)],
                r_in.at[way, here.chip],
                here.at(y=turn_y[dy], z=turn_z[dz]),
            )
        r_in[way, here.chip] = results[way, here.chip]
        yield
        for dy, dz in reversed(apart):
            wires.arrived(("r", way, dy, dz), r_in.at[way, chip_at(-dy, -dz)])
        for i, h in enumerate(heads):
            s_even, s_odd = both_states(i)
            enters = jnp.stack([r_in[way, 2 * piece + i // 3, i % 3] for piece in range(8)], axis=0).astype(F32)
            if way == 0:
                at_even, at_odd = enters, s_even + jnp.exp(log_total(even, h)) * enters
            else:
                at_even, at_odd = s_odd + jnp.exp(log_total(odd, h)) * enters, enters
            for_sib[way, i] = jnp.where(core == 0, at_odd, at_even).astype(BF16)
            final[way, h] = jnp.where(core == 0, at_even, at_odd).astype(BF16)
        wires.send(("f", way), for_sib.at[way], final.at[way, pl.ds(core * HALF_HEADS, HALF_HEADS)], here.sibling())
        yield
        wires.arrived(("f", way), final.at[way, pl.ds(other * HALF_HEADS, HALF_HEADS)])
        yield

    for load in soon:
        load.wait()
    for h in range(HEADS):
        at = slice(h * HD, (h + 1) * HD)
        scaled[0, :, at] = (tails[:, h : h + 1] * k_ref[:, at].astype(F32)).astype(BF16)
        scaled[1, :, at] = (jnp.exp(turned[:, h : h + 1]) * q_ref[:, at].astype(F32)).astype(BF16)
    to_owner(2)
    earlier = scan(0, v_ref)
    next(earlier)

    first = jnp.where(core == 0, here.z, here.y)
    second = jnp.where(core == 0, here.y, here.z)
    first_step, second_step = jnp.where(core == 0, 1, 4), jnp.where(core == 0, 4, 1)
    fs = [lax.rem(first + d, 4) for d in range(4)]
    ss = [lax.rem(second + d, 4) for d in range(4)]

    def on_first(value):
        return here.at(y=jnp.where(core == 0, here.y, value), z=jnp.where(core == 0, value, here.z))

    def on_second(value):
        return here.at(y=jnp.where(core == 0, value, here.y), z=jnp.where(core == 0, here.z, value))

    own_pair = lax.div(here.x, 2)
    pairs = (own_pair, 1 - own_pair)

    def enter(turn):
        for d in ((1,), (2, 3))[turn]:
            wires.arrived(("x", d), mine.at[own_rows, quarter_at(across[d])])
            wires.arrived(("xr", d), ninth_in.at[across[d]])
        p = pairs[turn]
        rows[core, own_rows, pl.ds(aligned(p * PAIR + 2 * QUARTER, 128), 384)] = (
            ninth_in[2 * p].astype(F32) + ninth_in[2 * p + 1].astype(F32)
        ).astype(BF16)

    def gather(turn):
        base = pairs[turn] * PAIR
        full = pl.ds(aligned(base, 128), PAIR)
        left = pl.ds(aligned(base, 128), PAIR_CUT)
        right = pl.ds(aligned(base + PAIR_CUT, 128), PAIR - PAIR_CUT)

        def tile(i, j, columns=full):
            at = (fs[i] * first_step + ss[j] * second_step) * 16
            return rows.at[core, pl.ds(aligned(at, 16), 16), columns]

        def send(name, region, device):
            wires.send((turn,) + name, region, region, device)

        def arrived(name, region):
            wires.arrived((turn,) + name, region)

        def share(i, j):
            send(("c", i, j), tile(i, j), here.sibling())

        def spread_second(i):
            send(("s+", i), tile(i, 0), on_second(ss[1]))
            send(("s-", i), tile(i, 0), on_second(ss[3]))
            share(i, 0)

        def pass_second(i):
            arrived(("s+", i), tile(i, 3))
            send(("s+l", i), tile(i, 3, left), on_second(ss[1]))
            share(i, 3)
            arrived(("s-", i), tile(i, 1))
            send(("s-r", i), tile(i, 1, right), on_second(ss[3]))
            share(i, 1)

        def end_second(i):
            arrived(("s+l", i), tile(i, 2, left))
            arrived(("s-r", i), tile(i, 2, right))
            share(i, 2)

        for d in (1, 3, 2):
            send(("f", d), tile(0, 0), on_first(fs[d]))
        spread_second(0)
        yield
        arrived(("f", 1), tile(3, 0))
        spread_second(3)
        arrived(("f", 3), tile(1, 0))
        spread_second(1)
        yield
        pass_second(0)
        yield
        arrived(("f", 2), tile(2, 0))
        spread_second(2)
        yield
        pass_second(3)
        yield
        pass_second(1)
        yield
        pass_second(2)
        yield
        end_second(0)
        yield
        end_second(3)
        yield
        end_second(1)
        yield
        end_second(2)
        yield
        for i in range(4):
            for j in range(4):
                at = (ss[i] * second_step + fs[j] * first_step) * 16
                arrived(("c", i, j), rows.at[other, pl.ds(aligned(at, 16), 16), full])
        yield

    enter(0)
    pull0, pull1 = gather(0), gather(1)
    next(pull0)
    enter(1)
    next(pull0)
    next(pull1)
    next(pull0)
    next(pull0)
    early_sends = len(wires.sent)
    next(pull0)
    next(pull0)
    next(pull1)
    next(pull0)
    next(pull1)
    next(pull1)
    for d in (1, 2, 3):
        wires.arrived(("dz", d), decay.at[pl.ds((here.y * 4 + turn_z[4 - d]) * 2, 2)])
    line_of_blocks = decay.at[pl.ds(here.y * 8, 8)]
    for d in (1, 2, 3):
        wires.send(("dy", d), line_of_blocks, line_of_blocks, here.at(y=turn_y[d]))
    next(pull0)
    next(pull0)
    next(pull0)
    next(pull1)
    next(pull1)
    next(pull0)
    next(pull1)
    wires.drain(early_sends)
    next(pull0)

    r0, r1 = iota((MAIN, MAIN), 0), iota((MAIN, MAIN), 1)

    def unfold(turn):
        chip_core, grp = lax.rem(r0, 32), lax.div(r0, 32)
        select = jnp.where(r1 == chip_core * 8 + grp, 1.0, 0.0).astype(BF16)
        base = pairs[turn] * PAIR
        for which in range(2):
            spread = dot(select, rows[which, 0:MAIN, pl.ds(aligned(base + 2 * QUARTER, 128), 384)]).astype(BF16)
            for g in range(8):
                at = pl.ds(aligned(base + g * 384, 128), 384)
                rows[which, MAIN:SLOTS, at] = spread[32 * g : 32 * (g + 1), :]

    def contract(turn, start, stop):
        def one(j, _):
            at = pl.ds(aligned(pairs[turn] * PAIR + j * 1024, 128), 1024)
            to = pl.ds(aligned(pairs[turn] * 2 * QUARTER + j * 1024, 1024), 1024)
            acc[...] += dot(rows[0, :, at], wgu[to, :])
            acc_down[...] += dot_nt(rows[1, :, at], wd[:, to])
            return 0

        lax.fori_loop(start, stop, one, 0)

    def weight_grads(start, stop):
        for i in range(start, stop):
            at = slice(1024 * i + 384 * (i // 3), 1024 * (i + 1) + 384 * (i // 3))
            to = slice(1024 * i, 1024 * (i + 1))
            both = dot_tn(rows[0, :, at], acts[...])
            gate_out[to, :] = both[:, 0:HID].astype(BF16)
            up_out[to, :] = both[:, HID:].astype(BF16)
            down_out[:, to] = dot_tn(hidden[...], rows[1, :, at]).astype(BF16)

    for load in loads:
        load.wait()
    acc[...] = jnp.zeros_like(acc)
    acc_down[...] = jnp.zeros_like(acc_down)
    unfold(0)
    contract(0, 0, 1)
    next(pull1)
    next(pull1)
    contract(0, 1, 2)
    next(pull1)
    contract(0, 2, 3)
    next(pull1)
    for d in (1, 2, 3):
        wires.arrived(("dy", d), decay.at[pl.ds(turn_y[4 - d] * 8, 8)])
    next(earlier)
    next(pull1)
    unfold(1)
    contract(1, 0, 3)
    wires.drain()
    gate_pre, up_pre, hidden_grad = acc[:, 0:HID], acc[:, HID:], acc_down[...]
    sig = jax.nn.sigmoid(gate_pre)
    active = gate_pre * sig
    hidden[...] = (active * up_pre).astype(BF16)
    acts[:, 0:HID] = (hidden_grad * up_pre * sig * (1.0 + gate_pre * (1.0 - sig))).astype(BF16)
    acts[:, HID:] = (hidden_grad * active).astype(BF16)

    def slot_part(which, owner, chunk):
        y_step, z_step = jnp.where(owner == 0, 4, 1), jnp.where(owner == 0, 1, 4)
        part = parts[chunk]
        for j, q in enumerate(QUARTERS[chunk]):
            at = pl.ds(aligned(q * QUARTER + owner * 768, 768), 768)
            piece = dot_nt(acts[...], wgu[at, :]).astype(BF16)
            for k in range(16):
                to = ((k // 4) * y_step + (k % 4) * z_step) * 16
                part[which, pl.ds(aligned(to, 16), 16), 768 * j : 768 * (j + 1)] = piece[16 * k : 16 * (k + 1), :]
            for b in range(2):
                g = 2 * q + b
                fold[which, 32 * g : 32 * (g + 1), :] = piece[MAIN:, 384 * b : 384 * (b + 1)]
        if chunk == 2:
            position, inside = lax.div(r0, 16), lax.rem(r0, 16)
            chip = jnp.where(owner == 0, position, lax.rem(position, 4) * 4 + lax.div(position, 4))
            source = lax.rem(inside, 8) * 32 + chip * 2 + lax.div(inside, 8)
            refold = jnp.where(r1 == source, 1.0, 0.0).astype(BF16)
            part[which, :, 768:] = dot(refold, fold[which]).astype(BF16)

    def slots_for_sibling(chunk):
        slot_part(1, other, chunk)
        wires.send(("p", chunk), parts[chunk].at[1], theirs[chunk], here.sibling())

    def join(chunk):
        wires.arrived(("p", chunk), theirs[chunk])
        part, far = parts[chunk], theirs[chunk]

        def one(j, _):
            at = pl.ds(aligned(j * 16, 16), 16)
            part[0, at, :] = (part[0, at, :].astype(F32) + far[at, :].astype(F32)).astype(BF16)
            return 0

        lax.fori_loop(0, 16, one, 0)

    def ring_sum(tag, buffer, height, cut, places, device, in_a, in_b, in_m, in_p, result):
        cl, cr = pl.ds(0, cut), pl.ds(cut, in_m.shape[1] - cut)

        def block(i, columns):
            return buffer.at[pl.ds(aligned(places[i] * height, height), height), columns]

        def add_into(i, columns, arrived_ref):
            at = pl.ds(aligned(places[i] * height, height), height)
            buffer[at, columns] = (buffer[at, columns].astype(F32) + arrived_ref[...].astype(F32)).astype(BF16)

        up, down = device(places[1]), device(places[3])
        wires.send((tag, "a"), block(2, cl), in_a, up)
        wires.send((tag, "b"), block(2, cr), in_b, down)
        wires.send((tag, "mr"), block(1, cr), in_m.at[:, cr], up)
        wires.send((tag, "pl"), block(3, cl), in_p.at[:, cl], down)
        yield
        wires.arrived((tag, "a"), in_a)
        add_into(1, cl, in_a)
        wires.send((tag, "ml"), block(1, cl), in_m.at[:, cl], up)
        wires.arrived((tag, "b"), in_b)
        add_into(3, cr, in_b)
        wires.send((tag, "pr"), block(3, cr), in_p.at[:, cr], down)
        yield
        wires.arrived((tag, "mr"), in_m.at[:, cr])
        wires.arrived((tag, "pl"), in_p.at[:, cl])
        wires.arrived((tag, "ml"), in_m.at[:, cl])
        wires.arrived((tag, "pr"), in_p.at[:, cr])
        at = pl.ds(aligned(places[0] * height, height), height)
        result[...] = (buffer[at, :].astype(F32) + in_m[...].astype(F32) + in_p[...].astype(F32)).astype(BF16)
        yield

    def far_direct(tag, buffer, height, places, device, in_q, in_m, in_p, result):
        def block(i):
            return pl.ds(aligned(places[i] * height, height), height)

        for d, landing in ((2, in_q), (1, in_m), (3, in_p)):
            wires.send((tag, d), buffer.at[block(d), :], landing, device(places[d]))
        yield
        yield
        total = buffer[block(0), :].astype(F32)
        for d, landing in ((1, in_m), (3, in_p), (2, in_q)):
            wires.arrived((tag, d), landing)
            total = total + landing[...].astype(F32)
        result[...] = total.astype(BF16)
        yield

    def direct_sum(tag, buffer, places, device, landing, result):
        def block(i):
            return pl.ds(aligned(places[i] * 16, 16), 16)

        for d in (2, 1, 3):
            wires.send((tag, d), buffer.at[block(d), :], landing.at[d], device(places[d]))
        yield
        total = buffer[block(0), :].astype(F32)
        for d in (1, 3, 2):
            wires.arrived((tag, d), landing.at[d])
            total = total + landing[d].astype(F32)
        result[...] = total.astype(BF16)
        yield

    far = [
        ring_sum(
            ("f", n), parts[n].at[0], 64, CHUNK_CUTS[n], ss, on_second,
            in_as[n], in_bs[n], in_ms[n], in_ps[n], groups[n],
        )
        for n in range(2)
    ]
    far.append(far_direct(("f", 2), parts[2].at[0], 64, ss, on_second, in_as[2], in_ms[2], in_ps[2], groups[2]))
    near = [direct_sum(("n", n), groups[n], fs, on_first, landings[n], sums[n]) for n in range(3)]
    slots_for_sibling(0)
    slot_part(0, core, 0)
    slots_for_sibling(1)
    join(0)
    next(far[0])
    slot_part(0, core, 1)
    join(1)
    next(far[1])
    slots_for_sibling(2)
    slot_part(0, core, 2)
    next(far[0])
    join(2)
    next(far[2])
    next(far[1])
    next(far[0])
    next(near[0])
    next(far[2])
    next(far[1])
    next(near[1])
    next(far[2])
    next(near[2])
    next(near[0])
    next(near[1])
    next(near[2])
    wires.drain(len(wires.sent) - 9)
    own_back = pl.ds(aligned(here.x * 16, 16), 16)
    for q in range(4):
        n, j = ((0, 0), (1, 0), (1, 1), (2, 0))[q]
        outgoing[16 * q : 16 * (q + 1), :] = sums[n][:, 768 * j : 768 * (j + 1)]
    for d in (1, 2, 3):
        source = outgoing.at[pl.ds(aligned(across[d] * 16, 16), 16), :]
        wires.send(("b", d), source, back.at[core, own_back, 0:768], here.at(x=across[d]))
        wires.send(("br", d), sums[2].at[:, 768:], back.at[core, own_back, 768:], here.at(x=across[d]))
    back[core, own_back, 0:768] = outgoing[own_back, :]
    back[core, own_back, 768:] = sums[2][:, 768:]
    next(earlier)
    weight_grads(0, 2)
    for d in (1, 2, 3):
        source = pl.ds(aligned(across[d] * 16, 16), 16)
        wires.arrived(("b", d), back.at[core, source, 0:768])
        wires.arrived(("br", d), back.at[core, source, 768:])
    wires.send("bc", back.at[core], back.at[core], here.sibling())
    weight_grads(2, 3)
    wires.arrived("bc", back.at[other])

    for b in range(2):
        chosen = jnp.where(slot == 2 * here.x + b, ninth, 0.0)
        pick_back = jnp.concatenate([main, chosen], axis=0).astype(BF16)
        for h in range(2):
            at = h * 768 + b * 384
            source = jnp.concatenate([back[h, :, 384 * b : 384 * (b + 1)], back[h, :, 768:]], axis=0)
            attn[:, at : at + 384] = (
                out_grad_ref[:, at : at + 384].astype(F32) + dot_tn(pick_back, source)
            ).astype(BF16)

    later = scan(1, attn)
    next(later)
    next(earlier)
    next(later)
    next(earlier)

    lower = iota((ROWS, ROWS), 0) >= iota((ROWS, ROWS), 1)

    def within(h):
        at = slice(h * HD, (h + 1) * HD)
        q, k, v, g = q_ref[:, at], k_ref[:, at], v_ref[:, at], attn[:, at]
        front = turned[:, h : h + 1]
        spread = front - run[h : h + 1, :]
        w = jnp.where(lower, jnp.exp(jnp.where(lower, spread, 0.0)), 0.0)
        mixed = (dot_nt(g, v) * w).astype(BF16)
        scores = (dot_nt(q, k) * w).astype(BF16)
        state_in = final[0, h].reshape(HD, HD)
        dq[:, at] = (dot(mixed, k) + jnp.exp(front) * dot_nt(g, state_in)).astype(BF16)
        kept[0, :, at] = dot_tn(mixed, q)
        kept[1, :, at] = dot_tn(scores, g)

    for h in range(0, 6):
        within(h)
    next(later)
    for h in range(6, HEADS):
        within(h)
    weight_grads(3, 5)
    next(later)
    weight_grads(5, 6)
    next(later)
    state_out[...] = final[1]
    wires.drain()
    wires.check()


def last_kernel(
    gate_ref, up_ref, down_ref, dq_ref, kept_ref, state_ref, tail_ref, k_hbm, v_hbm,
    gate_hbm, up_hbm, down_hbm, dq_out, dk_out, dv_out,
    k_ref, v_ref, dk_ref, dv_ref, sems,
):
    copies = []

    def start(src, dst):
        copy = pltpu.make_async_copy(src, dst, sems.at[len(copies)])
        copy.start()
        copies.append(copy)
        return copy

    loads = [start(k_hbm, k_ref), start(v_hbm, v_ref)]
    stores = [
        start(src, dst)
        for src, dst in ((gate_ref, gate_hbm), (up_ref, up_hbm), (down_ref, down_hbm), (dq_ref, dq_out))
    ]
    for load in loads:
        load.wait()
    for h in range(HEADS):
        at = slice(h * HD, (h + 1) * HD)
        tail, state = tail_ref[:, h : h + 1], state_ref[h].reshape(HD, HD)
        dk_ref[:, at] = (kept_ref[0, :, at] + tail * dot_nt(v_ref[:, at], state)).astype(BF16)
        dv_ref[:, at] = (kept_ref[1, :, at] + tail * dot(k_ref[:, at], state)).astype(BF16)
    stores += [start(dk_ref, dk_out), start(dv_ref, dv_out)]
    for store in stores:
        store.wait()


def in_vmem(count):
    return [pl.BlockSpec(memory_space=pltpu.VMEM)] * count


def in_hbm(count):
    return [pl.BlockSpec(memory_space=pl.ANY)] * count


def shape(dims, kind=BF16):
    return jax.ShapeDtypeStruct(dims, kind)


def main_call(ids, route_gates, log_decay, moe_input, out_grad, queries, keys, values, w_gate, w_up, w_down):
    half = (2, HALF_HEADS, 8, 16, HD)
    piece = (2, 16, 3, 16, HD)
    wide = (2, HEADS, 8, 16, HD)

    bf16_scratch = (
        [(ROWS, QUARTER)] * 5
        + [(D, 2 * HID), (HID, D), (2, SLOTS, WIDE), (2, 64, QUARTER + 384), (64, QUARTER + 384), (4, 16, 384)],
        [(SLOTS, HID), (SLOTS, 2 * HID)]
        + [(2, MAIN, 384), (64, 768), (2, 64, 1152)],
        [(2, ROWS, QUARTER), (ROWS, QUARTER), wide, half, piece, piece, piece, piece, half, wide],
    )
    f32_scratch = (
        [(SLOTS, 2 * HID), (SLOTS, HID)],
        [(32, 16, ROWS), (16, ROWS), (ROWS, ROWS)],
        [],
    )
    scratch = [pltpu.VMEM((2, ROWS), jnp.int32), pltpu.VMEM((2, ROWS), F32), pltpu.VMEM((HEADS, ROWS), F32)]
    for narrow, broad in zip(bf16_scratch, f32_scratch):
        scratch += [pltpu.VMEM(dims, BF16) for dims in narrow]
        scratch += [pltpu.VMEM(dims, F32) for dims in broad]
    for n, (width, cut) in enumerate(zip(CHUNKS, CHUNK_CUTS)):
        firsts = ((64, cut), (64, width - cut)) if n < 2 else ((64, width), (16, 128))
        for dims in (
            (2, MAIN, width), (MAIN, width), *firsts, (64, width), (64, width),
            (64, width), (4, 16, width), (16, width),
        ):
            scratch.append(pltpu.VMEM(dims, BF16))
    return pl.pallas_call(
        main_kernel,
        out_shape=(
            pltpu.VMEM((D, HID), BF16),
            pltpu.VMEM((D, HID), BF16),
            pltpu.VMEM((HID, D), BF16),
            pltpu.VMEM((ROWS, QUARTER), BF16),
            pltpu.VMEM((2, ROWS, QUARTER), F32),
            pltpu.VMEM((HEADS, 8, 16, HD), BF16),
            pltpu.VMEM((ROWS, ROWS), F32),
        ),
        in_specs=[pl.BlockSpec(memory_space=pltpu.HBM)] * 11,
        out_specs=tuple(in_vmem(7)),
        scratch_shapes=scratch
        + [
            pltpu.SemaphoreType.DMA((SENDS,)),
            pltpu.SemaphoreType.DMA((RECEIVES,)),
            pltpu.SemaphoreType.DMA((11,)),
        ],
        compiler_params=pltpu.CompilerParams(collective_id=0, has_side_effects=True, vmem_limit_bytes=BIG),
        name="routed_experts_and_scans",
    )(
        *(
            pltpu.with_memory_space_constraint(a, pltpu.HBM)
            for a in (
                ids, route_gates, log_decay, moe_input, out_grad, queries, keys, values, w_gate, w_up, w_down
            )
        )
    )


def last_call(gate_grad, up_grad, down_grad, dq, kept, state, tails, keys, values):
    held = (gate_grad, up_grad, down_grad, dq, kept, state, tails)
    outputs = [(D, HID), (D, HID), (HID, D), (ROWS, QUARTER), (ROWS, QUARTER), (ROWS, QUARTER)]
    return pl.pallas_call(
        last_kernel,
        out_shape=tuple(shape(dims) for dims in outputs),
        in_specs=in_vmem(7) + [pl.BlockSpec(memory_space=pltpu.HBM)] * 2,
        out_specs=tuple(in_hbm(len(outputs))),
        scratch_shapes=[pltpu.VMEM((ROWS, QUARTER), BF16)] * 4 + [pltpu.SemaphoreType.DMA((8,))],
        compiler_params=pltpu.CompilerParams(vmem_limit_bytes=16 * 1024 * 1024),
        name="outputs",
    )(*(pltpu.with_memory_space_constraint(a, pltpu.VMEM) for a in held), keys, values)


def on_device(
    queries, keys, values, log_decay, moe_input, out_grad, expert_ids, route_gates, w_gate, w_up, w_down
):
    held = main_call(
        expert_ids.T, route_gates.T, log_decay, moe_input, out_grad, queries, keys, values, w_gate[0], w_up[0], w_down[0]
    )
    gate_part, up_part, down_part, query_grad, key_grad, value_grad = last_call(*held, keys, values)
    return (query_grad, key_grad, value_grad, gate_part[None], up_part[None], down_part[None])


def solution(mesh):
    rows, heads = P("ctx", "exp"), P("exp", "ctx")
    columns, down = P("exp", None, "ctx"), P("exp", "ctx", None)
    return jax.shard_map(
        on_device,
        mesh=mesh,
        in_specs=(rows, rows, rows, heads, rows, rows, P("ctx", None), P("ctx", None), columns, columns, down),
        out_specs=(rows, rows, rows, columns, columns, down),
        check_vma=False,
    )
```

```python
import jax
import jax.numpy as jnp
from jax import lax
from jax.experimental import pallas as pl
from jax.experimental.pallas import tpu as pltpu
from jax.sharding import PartitionSpec as P

MESH = pl.DeviceIdType.MESH
BF16 = jnp.bfloat16
F32 = jnp.float32

FLIGHT = 4
D = 6144
QUARTER = D // 4
HID = 256
HEADS = 12
HALF_HEADS = HEADS // 2
HD = 128
ROWS = 128
MAIN = 256
SLOTS = 288
PAIR = 2 * QUARTER + 384
PAIR_CUT = 1792
WIDE = 2 * PAIR
QUARTERS = ((0,), (1, 2), (3,))
CHUNKS = (768, 1536, 1152)
CHUNK_CUTS = (384, 768, 640)
SENDS = 77
RECEIVES = 182
BIG = 42 * 1024 * 1024


def dot(a, b):
    return lax.dot_general(a, b, (((1,), (0,)), ((), ())), preferred_element_type=F32)


def dot_nt(a, b):
    return lax.dot_general(a, b, (((1,), (1,)), ((), ())), preferred_element_type=F32)


def dot_tn(a, b):
    return lax.dot_general(a, b, (((0,), (0,)), ((), ())), preferred_element_type=F32)


def iota(shape, dim):
    return lax.broadcasted_iota(jnp.int32, shape, dim)


def aligned(value, by):
    return pl.multiple_of(value, by)


class Place:
    def __init__(self):
        ctx = lax.axis_index("ctx")
        self.x = lax.axis_index("exp")
        self.ctx = ctx
        self.core = lax.rem(ctx, 2)
        self.z = lax.rem(lax.div(ctx, 2), 4)
        self.y = lax.div(ctx, 8)
        self.chip = self.y * 4 + self.z

    def at(self, y=None, z=None, core=None, x=None):
        y = self.y if y is None else y
        z = self.z if z is None else z
        core = self.core if core is None else core
        x = self.x if x is None else x
        return (y * 8 + z * 2 + core, x)

    def sibling(self):
        return self.at(core=1 - self.core)


class Wires:
    def __init__(self, place, send_sems, recv_sems):
        self.place, self.send_sems, self.recv_sems = place, send_sems, recv_sems
        self.names, self.sent, self.free, self.most = {}, [], [], 0

    def slot(self, name):
        return self.names.setdefault(name, len(self.names))

    def send(self, name, src, dst, device):
        if not self.free:
            self.free, self.most = [self.most], self.most + 1
        semaphore = self.free.pop()
        copy = pltpu.make_async_remote_copy(
            src_ref=src,
            dst_ref=dst,
            send_sem=self.send_sems.at[semaphore],
            recv_sem=self.recv_sems.at[self.slot(name)],
            device_id=device,
            device_id_type=MESH,
        )
        copy.start()
        self.sent.append((copy, semaphore))

    def arrived(self, name, region):
        pltpu.make_async_remote_copy(
            src_ref=region,
            dst_ref=region,
            send_sem=self.send_sems.at[0],
            recv_sem=self.recv_sems.at[self.slot(name)],
            device_id=self.place.sibling(),
            device_id_type=MESH,
        ).wait_recv()

    def drain(self, count=None):
        count = len(self.sent) if count is None else count
        for copy, semaphore in self.sent[:count]:
            copy.wait_send()
            self.free.append(semaphore)
        self.sent = self.sent[count:]

    def check(self):
        assert self.most == SENDS and len(self.names) == RECEIVES, (self.most, len(self.names))


def greet(devices):
    for device in devices:
        pl.semaphore_signal(pltpu.get_barrier_semaphore(), inc=1, device_id=device, device_id_type=MESH)


def greeted(count):
    pl.semaphore_wait(pltpu.get_barrier_semaphore(), count)


def route_masks(ids, route_gates, place):
    wanted = iota((8, ROWS), 0)
    first = ids[0:1, :] == wanted
    second = ids[1:2, :] == wanted
    onehot = jnp.where(first | second, 1.0, 0.0)
    gates = jnp.where(first, route_gates[0:1, :], 0.0) + jnp.where(second, route_gates[1:2, :], 0.0)
    before = jnp.where(iota((ROWS, ROWS), 0) < iota((ROWS, ROWS), 1), 1.0, 0.0).astype(BF16)
    rank = dot(onehot.astype(BF16), before)
    rank = jnp.where(onehot > 0.5, rank, -1.0)

    def spread(a):
        return jnp.concatenate([jnp.broadcast_to(a[e : e + 1, :], (16, ROWS)) for e in range(FLIGHT)], axis=0)

    rank, gates = spread(rank), spread(gates)
    row = lax.rem(iota((64, ROWS), 0), 16)
    mine = lax.div(row, 8) == place.core
    slot = lax.rem(row, 8)
    main = jnp.where(mine & (rank == slot.astype(F32)), 1.0, 0.0)
    ninth = jnp.where(mine & (rank == 8.0), 1.0, 0.0)
    return main, ninth, slot, gates


def main_kernel(
    ids_hbm, route_gates_hbm, log_decay_hbm, moe_hbm, out_grad_hbm, q_hbm, k_hbm, v_hbm, wg_hbm, wu_hbm, wd_hbm,
    gate_out, up_out, down_out, dq, kept, state_out, tails,
    ids_ref, route_gates_ref, log_decay_ref,
    moe_ref, out_grad_ref, q_ref, k_ref, v_ref, wgu, wd, rows, stage, staged, ninth_in, acc, acc_down, hidden, acts,
    fold,
    outgoing, back, decay, run, turned, scaled, attn,
    states, sib, totals, t_in, results, r_in, for_sib, final,
    *rest,
):
    send_sems, recv_sems, local_sems = rest[-3:]
    parts, theirs, in_as, in_bs, in_ms, in_ps, groups, landings, sums = (
        rest[i : len(rest) - 3 : 9] for i in range(9)
    )
    here = Place()
    core, other = here.core, 1 - here.core
    wires = Wires(here, send_sems, recv_sems)
    def local_copy(src, dst, index):
        copy = pltpu.make_async_copy(src, dst, local_sems.at[index])
        copy.start()
        return copy

    across = [here.x, here.x + 1 - 2 * lax.rem(here.x, 2), lax.rem(here.x + 2, 4), 3 - here.x]
    turn_y = [lax.rem(here.y + d, 4) for d in range(4)]
    turn_z = [lax.rem(here.z + d, 4) for d in range(4)]
    tiny = [
        local_copy(log_decay_hbm, log_decay_ref, 0),
        local_copy(ids_hbm, ids_ref, 1),
        local_copy(route_gates_hbm, route_gates_ref, 2),
    ]
    early = [local_copy(moe_hbm, moe_ref, 3), local_copy(out_grad_hbm, out_grad_ref, 4)]
    greet(
        [here.sibling()]
        + [here.at(x=across[d]) for d in (1, 2, 3)]
        + [here.at(y=turn_y[dy], z=turn_z[dz]) for dy in range(4) for dz in range(4) if dy or dz]
    )
    soon = [local_copy(k_hbm, k_ref, 5), local_copy(q_hbm, q_ref, 6), local_copy(v_hbm, v_ref, 7)]
    loads = [
        local_copy(wg_hbm, wgu.at[:, 0:HID], 8),
        local_copy(wu_hbm, wgu.at[:, HID:], 9),
        local_copy(wd_hbm, wd, 10),
    ]
    for load in tiny:
        load.wait()

    run[...] = jnp.zeros_like(run)
    run[0:HEADS, :] = log_decay_ref[...]
    log_decay = run[...]
    decay[here.ctx] = jnp.broadcast_to(jnp.sum(log_decay, axis=1, keepdims=True), (16, ROWS))

    main, ninth, slot, gates = route_masks(ids_ref[...], route_gates_ref[...], here)
    pick = main.astype(BF16)
    main_gate = jnp.sum(main * gates, axis=1, keepdims=True)
    ninth_gate = jnp.sum(ninth * gates, axis=1, keepdims=True)
    fold_at = lax.rem(here.x, 2) * 4
    for load in early:
        load.wait()
    picks = [jnp.where(slot == fold_at + b, ninth, 0.0).astype(BF16) for b in range(4)]
    for which, source in enumerate((moe_ref, out_grad_ref)):
        chosen = dot(pick, source[...])
        extra = dot(picks[0], source[:, 0:384])
        for b in range(1, 4):
            extra = extra + dot(picks[b], source[:, 384 * b : 384 * (b + 1)])
        if which:
            chosen, extra = chosen * main_gate, extra * ninth_gate
        stage[which, :, 0:QUARTER] = chosen.astype(BF16)
        stage[which, :, QUARTER:] = extra.astype(BF16)
    greeted(19)
    wires.send("s", stage.at[other], staged, here.sibling())
    wires.send("d", decay.at[here.ctx], decay.at[here.ctx], here.sibling())

    lane = iota((16, ROWS), 1)
    step = 1
    while step < ROWS:
        log_decay = log_decay + jnp.where(lane >= step, pltpu.roll(log_decay, step, 1), 0.0)
        step *= 2
    run[...] = log_decay
    turned[...] = jnp.concatenate([log_decay, jnp.zeros((ROWS - 16, ROWS), F32)], axis=0).T
    ends = jnp.concatenate(
        [jnp.broadcast_to(log_decay[:, ROWS - 1 :], (16, ROWS)), jnp.zeros((ROWS - 16, ROWS), F32)], axis=0
    ).T
    tails[...] = jnp.exp(ends - turned[...])

    wires.arrived("s", staged)
    stage[core] = (stage[core].astype(F32) + staged[...].astype(F32)).astype(BF16)

    mine = rows.at[core]
    own_rows = pl.ds(aligned(here.chip * 16, 16), 16)

    def quarter_at(x):
        return pl.ds(aligned(lax.div(x, 2) * PAIR + lax.rem(x, 2) * QUARTER, 128), QUARTER)

    def to_owner(d):
        to = pl.ds(aligned(across[d] * 16, 16), 16)
        wires.send(
            ("x", d), stage.at[core, to, 0:QUARTER], mine.at[own_rows, quarter_at(here.x)], here.at(x=across[d])
        )
        wires.send(("xr", d), stage.at[core, to, QUARTER:], ninth_in.at[here.x], here.at(x=across[d]))

    to_owner(1)
    to_owner(3)
    to = pl.ds(aligned(here.x * 16, 16), 16)
    rows[core, own_rows, quarter_at(here.x)] = stage[core, to, 0:QUARTER]
    ninth_in[here.x] = stage[core, to, QUARTER:]

    wires.arrived("d", decay.at[here.at(core=other)[0]])
    pair_of_blocks = decay.at[pl.ds(here.chip * 2, 2)]
    for d in (1, 2, 3):
        wires.send(("dz", d), pair_of_blocks, pair_of_blocks, here.at(z=turn_z[d]))

    def log_total(block, h):
        return decay[block, pl.ds(h, 1), :]

    even, odd = here.chip * 2, here.chip * 2 + 1

    apart = [(dy, dz) for dy in (2, 1, 3, 0) for dz in (2, 1, 3, 0) if dy or dz]

    def chip_at(dy, dz):
        return turn_y[dy % 4] * 4 + turn_z[dz % 4]

    def scan(way, source):
        heads = [core * HALF_HEADS + i for i in range(HALF_HEADS)]
        order = range(16) if way == 0 else range(15, -1, -1)

        def own_states(half):
            for i in range(HALF_HEADS):
                h = half * HALF_HEADS + i
                at = pl.ds(aligned(h * HD, HD), HD)
                states[way, h] = dot_tn(scaled[way, :, at], source[:, at]).astype(BF16).reshape(8, 16, HD)

        def both_states(i):
            own, far = states[way, heads[i]].astype(F32), sib[way, i].astype(F32)
            return jnp.where(core == 0, own, far), jnp.where(core == 0, far, own)

        own_states(other)
        wires.send(("s", way), states.at[way, pl.ds(other * HALF_HEADS, HALF_HEADS)], sib.at[way], here.sibling())
        own_states(core)
        yield
        wires.arrived(("s", way), sib.at[way])
        for i, h in enumerate(heads):
            s_even, s_odd = both_states(i)
            if way == 0:
                whole = s_odd + jnp.exp(log_total(odd, h)) * s_even
            else:
                whole = s_even + jnp.exp(log_total(even, h)) * s_odd
            whole = whole.astype(BF16)
            for piece in range(8):
                totals[way, 2 * piece + i // 3, i % 3] = whole[piece]
        for dy, dz in apart:
            wires.send(
                ("t", way, dy, dz),
                totals.at[way, chip_at(dy, dz)],
                t_in.at[way, here.chip],
                here.at(y=turn_y[dy], z=turn_z[dz]),
            )
        t_in[way, here.chip] = totals[way, here.chip]
        yield
        for dy, dz in reversed(apart):
            wires.arrived(("t", way, dy, dz), t_in.at[way, chip_at(-dy, -dz)])
        for i in range(3):
            h = core * HALF_HEADS + 3 * lax.rem(here.chip, 2) + i
            total = jnp.zeros((16, HD), F32)
            for n in order:
                results[way, n, i] = total.astype(BF16)
                decayed = jnp.exp(log_total(2 * n, h) + log_total(2 * n + 1, h))
                total = t_in[way, n, i].astype(F32) + decayed * total
        for dy, dz in apart:
            wires.send(
                ("r", way, dy, dz),
                results.at[way, chip_at(dy, dz)],
                r_in.at[way, here.chip],
                here.at(y=turn_y[dy], z=turn_z[dz]),
            )
        r_in[way, here.chip] = results[way, here.chip]
        yield
        for dy, dz in reversed(apart):
            wires.arrived(("r", way, dy, dz), r_in.at[way, chip_at(-dy, -dz)])
        for i, h in enumerate(heads):
            s_even, s_odd = both_states(i)
            enters = jnp.stack([r_in[way, 2 * piece + i // 3, i % 3] for piece in range(8)], axis=0).astype(F32)
            if way == 0:
                at_even, at_odd = enters, s_even + jnp.exp(log_total(even, h)) * enters
            else:
                at_even, at_odd = s_odd + jnp.exp(log_total(odd, h)) * enters, enters
            for_sib[way, i] = jnp.where(core == 0, at_odd, at_even).astype(BF16)
            final[way, h] = jnp.where(core == 0, at_even, at_odd).astype(BF16)
        wires.send(("f", way), for_sib.at[way], final.at[way, pl.ds(core * HALF_HEADS, HALF_HEADS)], here.sibling())
        yield
        wires.arrived(("f", way), final.at[way, pl.ds(other * HALF_HEADS, HALF_HEADS)])
        yield

    for load in soon:
        load.wait()
    for h in range(HEADS):
        at = slice(h * HD, (h + 1) * HD)
        scaled[0, :, at] = (tails[:, h : h + 1] * k_ref[:, at].astype(F32)).astype(BF16)
        scaled[1, :, at] = (jnp.exp(turned[:, h : h + 1]) * q_ref[:, at].astype(F32)).astype(BF16)
    to_owner(2)
    earlier = scan(0, v_ref)
    next(earlier)

    first = jnp.where(core == 0, here.z, here.y)
    second = jnp.where(core == 0, here.y, here.z)
    first_step, second_step = jnp.where(core == 0, 1, 4), jnp.where(core == 0, 4, 1)
    fs = [lax.rem(first + d, 4) for d in range(4)]
    ss = [lax.rem(second + d, 4) for d in range(4)]

    def on_first(value):
        return here.at(y=jnp.where(core == 0, here.y, value), z=jnp.where(core == 0, value, here.z))

    def on_second(value):
        return here.at(y=jnp.where(core == 0, value, here.y), z=jnp.where(core == 0, here.z, value))

    own_pair = lax.div(here.x, 2)
    pairs = (own_pair, 1 - own_pair)

    def enter(turn):
        for d in ((1,), (2, 3))[turn]:
            wires.arrived(("x", d), mine.at[own_rows, quarter_at(across[d])])
            wires.arrived(("xr", d), ninth_in.at[across[d]])
        p = pairs[turn]
        rows[core, own_rows, pl.ds(aligned(p * PAIR + 2 * QUARTER, 128), 384)] = (
            ninth_in[2 * p].astype(F32) + ninth_in[2 * p + 1].astype(F32)
        ).astype(BF16)

    def gather(turn):
        base = pairs[turn] * PAIR
        full = pl.ds(aligned(base, 128), PAIR)
        left = pl.ds(aligned(base, 128), PAIR_CUT)
        right = pl.ds(aligned(base + PAIR_CUT, 128), PAIR - PAIR_CUT)

        def tile(i, j, columns=full):
            at = (fs[i] * first_step + ss[j] * second_step) * 16
            return rows.at[core, pl.ds(aligned(at, 16), 16), columns]

        def send(name, region, device):
            wires.send((turn,) + name, region, region, device)

        def arrived(name, region):
            wires.arrived((turn,) + name, region)

        def share(i, j):
            send(("c", i, j), tile(i, j), here.sibling())

        def spread_second(i):
            send(("s+", i), tile(i, 0), on_second(ss[1]))
            send(("s-", i), tile(i, 0), on_second(ss[3]))
            share(i, 0)

        def pass_second(i):
            arrived(("s+", i), tile(i, 3))
            send(("s+l", i), tile(i, 3, left), on_second(ss[1]))
            share(i, 3)
            arrived(("s-", i), tile(i, 1))
            send(("s-r", i), tile(i, 1, right), on_second(ss[3]))
            share(i, 1)

        def end_second(i):
            arrived(("s+l", i), tile(i, 2, left))
            arrived(("s-r", i), tile(i, 2, right))
            share(i, 2)

        for d in (1, 3, 2):
            send(("f", d), tile(0, 0), on_first(fs[d]))
        spread_second(0)
        yield
        arrived(("f", 1), tile(3, 0))
        spread_second(3)
        arrived(("f", 3), tile(1, 0))
        spread_second(1)
        yield
        pass_second(0)
        yield
        arrived(("f", 2), tile(2, 0))
        spread_second(2)
        yield
        pass_second(3)
        yield
        pass_second(1)
        yield
        pass_second(2)
        yield
        end_second(0)
        yield
        end_second(3)
        yield
        end_second(1)
        yield
        end_second(2)
        yield
        for i in range(4):
            for j in range(4):
                at = (ss[i] * second_step + fs[j] * first_step) * 16
                arrived(("c", i, j), rows.at[other, pl.ds(aligned(at, 16), 16), full])
        yield

    enter(0)
    pull0, pull1 = gather(0), gather(1)
    next(pull0)
    enter(1)
    next(pull1)
    next(pull0)
    next(pull0)
    next(pull0)
    early_sends = len(wires.sent)
    next(pull0)
    next(pull0)
    next(pull1)
    next(pull0)
    next(pull1)
    next(pull1)
    for d in (1, 2, 3):
        wires.arrived(("dz", d), decay.at[pl.ds((here.y * 4 + turn_z[4 - d]) * 2, 2)])
    line_of_blocks = decay.at[pl.ds(here.y * 8, 8)]
    for d in (1, 2, 3):
        wires.send(("dy", d), line_of_blocks, line_of_blocks, here.at(y=turn_y[d]))
    next(pull0)
    next(pull0)
    next(pull0)
    next(pull1)
    next(pull1)
    next(pull0)
    wires.drain(early_sends)
    next(pull0)

    r0, r1 = iota((MAIN, MAIN), 0), iota((MAIN, MAIN), 1)

    def unfold(turn, which):
        chip_core, grp = lax.rem(r0, 32), lax.div(r0, 32)
        select = jnp.where(r1 == chip_core * 8 + grp, 1.0, 0.0).astype(BF16)
        base = pairs[turn] * PAIR
        spread = dot(select, rows[which, 0:MAIN, pl.ds(aligned(base + 2 * QUARTER, 128), 384)]).astype(BF16)
        for g in range(8):
            at = pl.ds(aligned(base + g * 384, 128), 384)
            rows[which, MAIN:SLOTS, at] = spread[32 * g : 32 * (g + 1), :]

    def depth(turn, j):
        at = pl.ds(aligned(pairs[turn] * PAIR + j * 1024, 128), 1024)
        return at, pl.ds(aligned(pairs[turn] * 2 * QUARTER + j * 1024, 1024), 1024)

    def contract_inputs(turn, start=0, stop=3):
        def one(j, _):
            at, to = depth(turn, j)
            acc[...] += dot(rows[0, :, at], wgu[to, :])
            return 0

        lax.fori_loop(start, stop, one, 0)

    def contract_grads(turn, start=0, stop=3):
        def one(j, _):
            at, to = depth(turn, j)
            acc_down[...] += dot_nt(rows[1, :, at], wd[:, to])
            return 0

        lax.fori_loop(start, stop, one, 0)

    def contract(turn, start, stop):
        contract_inputs(turn, start, stop)
        contract_grads(turn, start, stop)

    def weight_grads(start, stop):
        for i in range(start, stop):
            at = slice(1024 * i + 384 * (i // 3), 1024 * (i + 1) + 384 * (i // 3))
            to = slice(1024 * i, 1024 * (i + 1))
            both = dot_tn(rows[0, :, at], acts[...])
            gate_out[to, :] = both[:, 0:HID].astype(BF16)
            up_out[to, :] = both[:, HID:].astype(BF16)
            down_out[:, to] = dot_tn(hidden[...], rows[1, :, at]).astype(BF16)

    for load in loads:
        load.wait()
    acc[...] = jnp.zeros_like(acc)
    acc_down[...] = jnp.zeros_like(acc_down)
    unfold(0, 0)
    unfold(0, 1)
    contract(0, 0, 1)
    next(pull1)
    contract(0, 1, 2)
    next(pull1)
    next(pull1)
    next(pull1)
    contract(0, 2, 3)
    next(pull1)
    for d in (1, 2, 3):
        wires.arrived(("dy", d), decay.at[pl.ds(turn_y[4 - d] * 8, 8)])
    next(earlier)
    unfold(1, core)
    pl.when(core == 0)(lambda: contract_inputs(1))
    pl.when(core == 1)(lambda: contract_grads(1))
    next(pull1)
    unfold(1, other)
    pl.when(core == 0)(lambda: contract_grads(1))
    pl.when(core == 1)(lambda: contract_inputs(1))
    wires.drain()
    gate_pre, up_pre, hidden_grad = acc[:, 0:HID], acc[:, HID:], acc_down[...]
    sig = jax.nn.sigmoid(gate_pre)
    active = gate_pre * sig
    hidden[...] = (active * up_pre).astype(BF16)
    acts[:, 0:HID] = (hidden_grad * up_pre * sig * (1.0 + gate_pre * (1.0 - sig))).astype(BF16)
    acts[:, HID:] = (hidden_grad * active).astype(BF16)

    def slot_part(which, owner, chunk):
        y_step, z_step = jnp.where(owner == 0, 4, 1), jnp.where(owner == 0, 1, 4)
        part = parts[chunk]
        for j, q in enumerate(QUARTERS[chunk]):
            at = pl.ds(aligned(q * QUARTER + owner * 768, 768), 768)
            piece = dot_nt(acts[...], wgu[at, :]).astype(BF16)
            for k in range(16):
                to = ((k // 4) * y_step + (k % 4) * z_step) * 16
                part[which, pl.ds(aligned(to, 16), 16), 768 * j : 768 * (j + 1)] = piece[16 * k : 16 * (k + 1), :]
            for b in range(2):
                g = 2 * q + b
                fold[which, 32 * g : 32 * (g + 1), :] = piece[MAIN:, 384 * b : 384 * (b + 1)]
        if chunk == 2:
            position, inside = lax.div(r0, 16), lax.rem(r0, 16)
            chip = jnp.where(owner == 0, position, lax.rem(position, 4) * 4 + lax.div(position, 4))
            source = lax.rem(inside, 8) * 32 + chip * 2 + lax.div(inside, 8)
            refold = jnp.where(r1 == source, 1.0, 0.0).astype(BF16)
            part[which, :, 768:] = dot(refold, fold[which]).astype(BF16)

    def slots_for_sibling(chunk):
        slot_part(1, other, chunk)
        wires.send(("p", chunk), parts[chunk].at[1], theirs[chunk], here.sibling())

    def join(chunk):
        wires.arrived(("p", chunk), theirs[chunk])
        part, far = parts[chunk], theirs[chunk]

        def one(j, _):
            at = pl.ds(aligned(j * 16, 16), 16)
            part[0, at, :] = (part[0, at, :].astype(F32) + far[at, :].astype(F32)).astype(BF16)
            return 0

        lax.fori_loop(0, 16, one, 0)

    def ring_sum(tag, buffer, height, cut, places, device, in_a, in_b, in_m, in_p, result):
        cl, cr = pl.ds(0, cut), pl.ds(cut, in_m.shape[1] - cut)

        def block(i, columns):
            return buffer.at[pl.ds(aligned(places[i] * height, height), height), columns]

        def add_into(i, columns, arrived_ref):
            at = pl.ds(aligned(places[i] * height, height), height)
            buffer[at, columns] = (buffer[at, columns].astype(F32) + arrived_ref[...].astype(F32)).astype(BF16)

        up, down = device(places[1]), device(places[3])
        wires.send((tag, "a"), block(2, cl), in_a, up)
        wires.send((tag, "b"), block(2, cr), in_b, down)
        wires.send((tag, "mr"), block(1, cr), in_m.at[:, cr], up)
        wires.send((tag, "pl"), block(3, cl), in_p.at[:, cl], down)
        yield
        wires.arrived((tag, "a"), in_a)
        add_into(1, cl, in_a)
        wires.send((tag, "ml"), block(1, cl), in_m.at[:, cl], up)
        wires.arrived((tag, "b"), in_b)
        add_into(3, cr, in_b)
        wires.send((tag, "pr"), block(3, cr), in_p.at[:, cr], down)
        yield
        wires.arrived((tag, "mr"), in_m.at[:, cr])
        wires.arrived((tag, "pl"), in_p.at[:, cl])
        wires.arrived((tag, "ml"), in_m.at[:, cl])
        wires.arrived((tag, "pr"), in_p.at[:, cr])
        at = pl.ds(aligned(places[0] * height, height), height)
        result[...] = (buffer[at, :].astype(F32) + in_m[...].astype(F32) + in_p[...].astype(F32)).astype(BF16)
        yield

    def far_direct(tag, buffer, height, places, device, in_q, in_m, in_p, result):
        def block(i):
            return pl.ds(aligned(places[i] * height, height), height)

        for d, landing in ((2, in_q), (1, in_m), (3, in_p)):
            wires.send((tag, d), buffer.at[block(d), :], landing, device(places[d]))
        yield
        yield
        total = buffer[block(0), :].astype(F32)
        for d, landing in ((1, in_m), (3, in_p), (2, in_q)):
            wires.arrived((tag, d), landing)
            total = total + landing[...].astype(F32)
        result[...] = total.astype(BF16)
        yield

    def direct_sum(tag, buffer, places, device, landing, result):
        def block(i):
            return pl.ds(aligned(places[i] * 16, 16), 16)

        for d in (2, 1, 3):
            wires.send((tag, d), buffer.at[block(d), :], landing.at[d], device(places[d]))
        yield
        total = buffer[block(0), :].astype(F32)
        for d in (1, 3, 2):
            wires.arrived((tag, d), landing.at[d])
            total = total + landing[d].astype(F32)
        result[...] = total.astype(BF16)
        yield

    far = [
        ring_sum(
            ("f", n), parts[n].at[0], 64, CHUNK_CUTS[n], ss, on_second,
            in_as[n], in_bs[n], in_ms[n], in_ps[n], groups[n],
        )
        for n in range(2)
    ]
    far.append(far_direct(("f", 2), parts[2].at[0], 64, ss, on_second, in_as[2], in_ms[2], in_ps[2], groups[2]))
    near = [direct_sum(("n", n), groups[n], fs, on_first, landings[n], sums[n]) for n in range(3)]
    slots_for_sibling(0)
    slot_part(0, core, 0)
    slots_for_sibling(1)
    join(0)
    next(far[0])
    slot_part(0, core, 1)
    join(1)
    next(far[1])
    slots_for_sibling(2)
    slot_part(0, core, 2)
    next(far[0])
    join(2)
    next(far[2])
    next(far[1])
    next(far[0])
    next(near[0])
    next(far[2])
    next(far[1])
    next(near[1])
    next(far[2])
    next(near[2])
    next(near[0])
    next(near[1])
    next(near[2])
    wires.drain(len(wires.sent) - 9)
    own_back = pl.ds(aligned(here.x * 16, 16), 16)
    for q in range(4):
        n, j = ((0, 0), (1, 0), (1, 1), (2, 0))[q]
        outgoing[16 * q : 16 * (q + 1), :] = sums[n][:, 768 * j : 768 * (j + 1)]
    for d in (1, 2, 3):
        source = outgoing.at[pl.ds(aligned(across[d] * 16, 16), 16), :]
        wires.send(("b", d), source, back.at[core, own_back, 0:768], here.at(x=across[d]))
        wires.send(("br", d), sums[2].at[:, 768:], back.at[core, own_back, 768:], here.at(x=across[d]))
    back[core, own_back, 0:768] = outgoing[own_back, :]
    back[core, own_back, 768:] = sums[2][:, 768:]
    next(earlier)
    weight_grads(0, 2)
    for d in (1, 2, 3):
        source = pl.ds(aligned(across[d] * 16, 16), 16)
        wires.arrived(("b", d), back.at[core, source, 0:768])
        wires.arrived(("br", d), back.at[core, source, 768:])
    wires.send("bc", back.at[core], back.at[core], here.sibling())
    weight_grads(2, 3)
    wires.arrived("bc", back.at[other])

    for b in range(2):
        chosen = jnp.where(slot == 2 * here.x + b, ninth, 0.0)
        pick_back = jnp.concatenate([main, chosen], axis=0).astype(BF16)
        for h in range(2):
            at = h * 768 + b * 384
            source = jnp.concatenate([back[h, :, 384 * b : 384 * (b + 1)], back[h, :, 768:]], axis=0)
            attn[:, at : at + 384] = (
                out_grad_ref[:, at : at + 384].astype(F32) + dot_tn(pick_back, source)
            ).astype(BF16)

    later = scan(1, attn)
    next(later)
    next(earlier)
    next(later)
    next(earlier)

    lower = iota((ROWS, ROWS), 0) >= iota((ROWS, ROWS), 1)

    def within(h):
        at = slice(h * HD, (h + 1) * HD)
        q, k, v, g = q_ref[:, at], k_ref[:, at], v_ref[:, at], attn[:, at]
        front = turned[:, h : h + 1]
        spread = front - run[h : h + 1, :]
        w = jnp.where(lower, jnp.exp(jnp.where(lower, spread, 0.0)), 0.0)
        mixed = (dot_nt(g, v) * w).astype(BF16)
        scores = (dot_nt(q, k) * w).astype(BF16)
        state_in = final[0, h].reshape(HD, HD)
        dq[:, at] = (dot(mixed, k) + jnp.exp(front) * dot_nt(g, state_in)).astype(BF16)
        kept[0, :, at] = dot_tn(mixed, q)
        kept[1, :, at] = dot_tn(scores, g)

    for h in range(0, 6):
        within(h)
    next(later)
    for h in range(6, HEADS):
        within(h)
    weight_grads(3, 5)
    next(later)
    weight_grads(5, 6)
    next(later)
    state_out[...] = final[1]
    wires.drain()
    wires.check()


def last_kernel(
    gate_ref, up_ref, down_ref, dq_ref, kept_ref, state_ref, tail_ref, k_hbm, v_hbm,
    gate_hbm, up_hbm, down_hbm, dq_out, dk_out, dv_out,
    k_ref, v_ref, dk_ref, dv_ref, sems,
):
    copies = []

    def start(src, dst):
        copy = pltpu.make_async_copy(src, dst, sems.at[len(copies)])
        copy.start()
        copies.append(copy)
        return copy

    loads = [start(k_hbm, k_ref), start(v_hbm, v_ref)]
    stores = [
        start(src, dst)
        for src, dst in ((gate_ref, gate_hbm), (up_ref, up_hbm), (down_ref, down_hbm), (dq_ref, dq_out))
    ]
    for load in loads:
        load.wait()
    for h in range(HEADS):
        at = slice(h * HD, (h + 1) * HD)
        tail, state = tail_ref[:, h : h + 1], state_ref[h].reshape(HD, HD)
        dk_ref[:, at] = (kept_ref[0, :, at] + tail * dot_nt(v_ref[:, at], state)).astype(BF16)
        dv_ref[:, at] = (kept_ref[1, :, at] + tail * dot(k_ref[:, at], state)).astype(BF16)
    stores += [start(dk_ref, dk_out), start(dv_ref, dv_out)]
    for store in stores:
        store.wait()


def in_vmem(count):
    return [pl.BlockSpec(memory_space=pltpu.VMEM)] * count


def in_hbm(count):
    return [pl.BlockSpec(memory_space=pl.ANY)] * count


def shape(dims, kind=BF16):
    return jax.ShapeDtypeStruct(dims, kind)


def main_call(ids, route_gates, log_decay, moe_input, out_grad, queries, keys, values, w_gate, w_up, w_down):
    half = (2, HALF_HEADS, 8, 16, HD)
    piece = (2, 16, 3, 16, HD)
    wide = (2, HEADS, 8, 16, HD)

    bf16_scratch = (
        [(ROWS, QUARTER)] * 5
        + [(D, 2 * HID), (HID, D), (2, SLOTS, WIDE), (2, 64, QUARTER + 384), (64, QUARTER + 384), (4, 16, 384)],
        [(SLOTS, HID), (SLOTS, 2 * HID)]
        + [(2, MAIN, 384), (64, 768), (2, 64, 1152)],
        [(2, ROWS, QUARTER), (ROWS, QUARTER), wide, half, piece, piece, piece, piece, half, wide],
    )
    f32_scratch = (
        [(SLOTS, 2 * HID), (SLOTS, HID)],
        [(32, 16, ROWS), (16, ROWS), (ROWS, ROWS)],
        [],
    )
    scratch = [pltpu.VMEM((2, ROWS), jnp.int32), pltpu.VMEM((2, ROWS), F32), pltpu.VMEM((HEADS, ROWS), F32)]
    for narrow, broad in zip(bf16_scratch, f32_scratch):
        scratch += [pltpu.VMEM(dims, BF16) for dims in narrow]
        scratch += [pltpu.VMEM(dims, F32) for dims in broad]
    for n, (width, cut) in enumerate(zip(CHUNKS, CHUNK_CUTS)):
        firsts = ((64, cut), (64, width - cut)) if n < 2 else ((64, width), (16, 128))
        for dims in (
            (2, MAIN, width), (MAIN, width), *firsts, (64, width), (64, width),
            (64, width), (4, 16, width), (16, width),
        ):
            scratch.append(pltpu.VMEM(dims, BF16))
    return pl.pallas_call(
        main_kernel,
        out_shape=(
            pltpu.VMEM((D, HID), BF16),
            pltpu.VMEM((D, HID), BF16),
            pltpu.VMEM((HID, D), BF16),
            pltpu.VMEM((ROWS, QUARTER), BF16),
            pltpu.VMEM((2, ROWS, QUARTER), F32),
            pltpu.VMEM((HEADS, 8, 16, HD), BF16),
            pltpu.VMEM((ROWS, ROWS), F32),
        ),
        in_specs=[pl.BlockSpec(memory_space=pltpu.HBM)] * 11,
        out_specs=tuple(in_vmem(7)),
        scratch_shapes=scratch
        + [
            pltpu.SemaphoreType.DMA((SENDS,)),
            pltpu.SemaphoreType.DMA((RECEIVES,)),
            pltpu.SemaphoreType.DMA((11,)),
        ],
        compiler_params=pltpu.CompilerParams(collective_id=0, has_side_effects=True, vmem_limit_bytes=BIG),
        name="routed_experts_and_scans",
    )(
        *(
            pltpu.with_memory_space_constraint(a, pltpu.HBM)
            for a in (
                ids, route_gates, log_decay, moe_input, out_grad, queries, keys, values, w_gate, w_up, w_down
            )
        )
    )


def last_call(gate_grad, up_grad, down_grad, dq, kept, state, tails, keys, values):
    held = (gate_grad, up_grad, down_grad, dq, kept, state, tails)
    outputs = [(D, HID), (D, HID), (HID, D), (ROWS, QUARTER), (ROWS, QUARTER), (ROWS, QUARTER)]
    return pl.pallas_call(
        last_kernel,
        out_shape=tuple(shape(dims) for dims in outputs),
        in_specs=in_vmem(7) + [pl.BlockSpec(memory_space=pltpu.HBM)] * 2,
        out_specs=tuple(in_hbm(len(outputs))),
        scratch_shapes=[pltpu.VMEM((ROWS, QUARTER), BF16)] * 4 + [pltpu.SemaphoreType.DMA((8,))],
        compiler_params=pltpu.CompilerParams(vmem_limit_bytes=16 * 1024 * 1024),
        name="outputs",
    )(*(pltpu.with_memory_space_constraint(a, pltpu.VMEM) for a in held), keys, values)


def on_device(
    queries, keys, values, log_decay, moe_input, out_grad, expert_ids, route_gates, w_gate, w_up, w_down
):
    held = main_call(
        expert_ids.T, route_gates.T, log_decay, moe_input, out_grad, queries, keys, values, w_gate[0], w_up[0], w_down[0]
    )
    gate_part, up_part, down_part, query_grad, key_grad, value_grad = last_call(*held, keys, values)
    return (query_grad, key_grad, value_grad, gate_part[None], up_part[None], down_part[None])


def solution(mesh):
    rows, heads = P("ctx", "exp"), P("exp", "ctx")
    columns, down = P("exp", None, "ctx"), P("exp", "ctx", None)
    return jax.shard_map(
        on_device,
        mesh=mesh,
        in_specs=(rows, rows, rows, heads, rows, rows, P("ctx", None), P("ctx", None), columns, columns, down),
        out_specs=(rows, rows, rows, columns, columns, down),
        check_vma=False,
    )
```
